1024 devices in a mesh: dom: 128 (over x, z, core), sub: 8 (over y).
Axes of the slice: x: 4, y: 8, z: 16, core: 2. Of those that a mesh axis runs over, the one named last changes fastest.
Arguments:
- solution: float32 [20, 9, 131072], P(None, None, ('dom', 'sub')), may hold values from -6 to 6
- geometry: float32 [7, 131072], P(None, ('dom', 'sub')), may hold values from 0.5 to 2
- cluster: int32 [131072], P(('dom', 'sub')), may hold values from 0 to 1, as said below
- neighbour: int32 [4, 131072], P(None, ('dom', 'sub')), may hold values from 0 to 255, as said below
- orient: int32 [4, 131072], P(None, ('dom', 'sub')), may hold values from 0 to 11
- send_elem: int32 [4, 32768], P(None, ('dom', 'sub')), may hold values from 0 to 127
- stiff_time: float32 [3, 20, 20], replicated, may hold values from -1.25 to 1.25
- stiff_vol: float32 [3, 20, 20], replicated, may hold values from -1.25 to 1.25
- jacobians: float32 [3, 9, 9], replicated, may hold values from -2 to 2
- flux_minus: float32 [4, 9, 9], replicated, may hold values from -2 to 2
- flux_plus: float32 [4, 9, 9], replicated, may hold values from -2 to 2
- lifting: float32 [4, 20, 10], replicated, may hold values from -2 to 2
- restrict: float32 [4, 10, 20], replicated, may hold values from -1.25 to 1.25
- orient_mat: float32 [3, 10, 10], replicated, may hold values from -2 to 2
Outputs:
- advanced: float32 [20, 9, 131072], P(None, None, ('dom', 'sub'))
The draws below stay inside these ranges and needn't reach their ends.
Inputs may be any that keep to these rules, and one draw needn't show every extreme that they name: `neighbour`: values below 128 are this device's elements; 128 + d * 32 + s names slot s received from direction d (0: the device one lower along dom, 1: one higher along dom, 2: one lower along sub, 3: one higher along sub). On each device every slot of a direction in which a device exists is named by exactly one face, and no slot of a direction without a device is named. On each device the elements of cluster 0 come first, at most 64 of them, and some device holds exactly 64.
All inputs are finite; a program needn't handle non-finite values.
Results may differ from the reference program's by a relative error of at most 0.0001.
Values sent between devices are 32-bit elements; how exact they have to be, the bound alone decides.
A program may use at most 32 MiB of HBM per device.

```python
import math
import jax
import jax.numpy as jnp
from jax import lax

E_DEV = 128
BASIS = 20
QUANT = 9
FACE_BASIS = 10
SLOTS = 32
FINE_CAP = 64
ELEMENTS = 131072
SEND_ROWS = 32768
N_DOM = 128
N_SUB = 8


def draw_neighbour(key, part):
    key = jax.random.fold_in(key, 3)
    devices = N_DOM * N_SUB
    faces = 4 * E_DEV
    device = jnp.arange(devices, dtype=jnp.int32)
    dom_index = device // N_SUB
    sub_index = device % N_SUB
    dev_keys = jax.random.split(jax.random.fold_in(key, 1), devices)
    shuffled = jax.vmap(lambda one_key: jax.random.permutation(one_key, faces))(dev_keys).astype(jnp.int32)
    ordinals = jnp.broadcast_to(jnp.arange(faces, dtype=jnp.int32)[None, :], (devices, faces))
    ranking = jnp.zeros((devices, faces), jnp.int32).at[device[:, None], shuffled].set(ordinals)
    present = jnp.stack([dom_index > 0, dom_index < N_DOM - 1, sub_index > 0, sub_index < N_SUB - 1], axis=1)
    direction = jnp.minimum(ranking // SLOTS, 3)
    is_ghost = (ranking < 4 * SLOTS) & jnp.take_along_axis(present, direction, axis=1)
    elem_id = jnp.arange(faces, dtype=jnp.int32) % E_DEV
    step_away = jax.random.randint(jax.random.fold_in(key, 2), (devices, faces), 1, E_DEV)
    local_rows = (elem_id[None, :] + step_away) % E_DEV
    chosen = jnp.where(is_ghost, E_DEV + ranking, local_rows).astype(jnp.int32)
    return chosen.reshape(devices, 4, E_DEV).transpose(1, 0, 2).reshape(4, devices * E_DEV)


def draw_cluster(key, part):
    key = jax.random.fold_in(key, 5)
    devices = N_DOM * N_SUB
    device = jnp.arange(devices, dtype=jnp.int32)
    fine_count = jax.random.randint(jax.random.fold_in(key, 1), (devices,), FINE_CAP // 8, FINE_CAP + 1)
    busiest = jax.random.randint(jax.random.fold_in(key, 2), (), 0, devices)
    fine_count = jnp.where(device == busiest, FINE_CAP, fine_count)
    elem_id = jnp.arange(E_DEV, dtype=jnp.int32)
    labels = (elem_id[None, :] >= fine_count[:, None]).astype(jnp.int32)
    return labels.reshape(devices * E_DEV)


def set_ends(entries, rng, smallest, largest):
    place = [jax.random.randint(jax.random.fold_in(rng, axis), (), 0, length) for axis, length in enumerate(entries.shape)]
    widest = entries.shape.index(max(entries.shape))
    beside = place[:widest] + [(place[widest] + 1) % entries.shape[widest]] + place[widest + 1:]
    return entries.at[tuple(place)].set(smallest).at[tuple(beside)].set(largest)


def shard_levels(stream_key, dims, pieces, smallest, largest):
    def one(position, shards_of):
        heights = jax.random.uniform(jax.random.fold_in(jax.random.fold_in(stream_key, 6), position), (shards_of,), jnp.float32, smallest / len(pieces), largest / len(pieces))
        return jnp.repeat(jnp.exp(heights), dims[position] // shards_of).reshape((-1,) + (1,) * (len(dims) - position - 1))

    level = one(*pieces[0])
    for cut in pieces[1:]:
        level = level * one(*cut)
    return level


def centred(rng, dims, scale, limit, cuts=(), kind=jnp.bfloat16):
    result = jax.random.normal(rng, dims, jnp.float32) * scale
    if len(cuts) > 0:
        result = shard_levels(rng, dims, cuts, -0.22, 0.18) * result
    return jnp.clip(result, min=-limit, max=limit).astype(kind)


def setup_inputs(seed: int = 0) -> dict:
    seeds = jax.random.split(jax.random.key(seed), 15)
    return {
        "solution": centred(seeds[0], (BASIS, QUANT, ELEMENTS), 1.0, 6.0, ((2, 1024),), jnp.float32),
        "geometry": jnp.clip(jnp.exp(math.log(2.0) - 1.3862944 * jax.random.uniform(seeds[1], (7, ELEMENTS), jnp.float32) ** shard_levels(seeds[1], (7, ELEMENTS), ((1, 1024),), -0.2, 0.2)), 0.5, 2.0),
        "cluster": draw_cluster(jax.random.fold_in(seeds[14], 71), 0),
        "neighbour": draw_neighbour(jax.random.fold_in(seeds[14], 71), 0),
        "orient": set_ends(jax.random.randint(seeds[4], (4, ELEMENTS), 0, 12), jax.random.fold_in(seeds[4], 1), 0, 11).astype(jnp.int32),
        "send_elem": set_ends(jax.random.randint(seeds[5], (4, SEND_ROWS), 0, E_DEV), jax.random.fold_in(seeds[5], 1), 0, E_DEV - 1).astype(jnp.int32),
        "stiff_time": centred(seeds[6], (3, BASIS, BASIS), BASIS ** -0.5, 1.25, (), jnp.float32),
        "stiff_vol": centred(seeds[7], (3, BASIS, BASIS), BASIS ** -0.5, 1.25, (), jnp.float32),
        "jacobians": centred(seeds[8], (3, QUANT, QUANT), QUANT ** -0.5, 2.0, (), jnp.float32),
        "flux_minus": centred(seeds[9], (4, QUANT, QUANT), QUANT ** -0.5, 2.0, (), jnp.float32),
        "flux_plus": centred(seeds[10], (4, QUANT, QUANT), QUANT ** -0.5, 2.0, (), jnp.float32),
        "lifting": centred(seeds[11], (4, BASIS, FACE_BASIS), FACE_BASIS ** -0.5, 2.0, (), jnp.float32),
        "restrict": centred(seeds[12], (4, FACE_BASIS, BASIS), BASIS ** -0.5, 1.25, (), jnp.float32),
        "orient_mat": centred(seeds[13], (3, FACE_BASIS, FACE_BASIS), FACE_BASIS ** -0.5, 2.0, (), jnp.float32),
    }


step_length = 0.4


def predict(values, scales, stiff_time, jacobians, spans):
    highest = lax.Precision.HIGHEST
    current = values
    sums = [(end_time - begin_time) * values for begin_time, end_time in spans]
    factorial = 1.0
    for degree in range(1, 4):
        summed = jnp.zeros(values.shape, jnp.float32)
        for dim_id in range(3):
            inner_sum = jnp.einsum('bc,cqe->bqe', stiff_time[dim_id], current, precision=highest)
            summed = summed + scales[dim_id] * jnp.einsum('bqe,qr->bre', inner_sum, jacobians[dim_id], precision=highest)
        current = -summed
        factorial = factorial * (degree + 1)
        sums = [partial_sum + ((end_time ** (degree + 1) - begin_time ** (degree + 1)) / factorial) * current
                for partial_sum, (begin_time, end_time) in zip(sums, spans)]
    return sums


def correct(own_part, sources, rows, orient, geometry, stiff_vol, jacobians, flux_minus, flux_plus, lifting, restrict, orient_mat):
    highest = lax.Precision.HIGHEST
    elements = own_part.shape[2]
    columns = sources.shape[2]
    traces = jnp.einsum('jbc,cqm->bqjm', restrict, sources, precision=highest)
    own_traces = traces[:, :, :, :elements]
    trace_flat = traces.reshape(traces.shape[0] * traces.shape[1], 4 * columns)
    positions = (orient // 3) * columns + rows
    gathered = jnp.take(trace_flat, positions, axis=1).reshape(traces.shape[0], traces.shape[1], 4, elements)
    rotation = orient % 3
    turned = jnp.zeros(gathered.shape, jnp.float32)
    for turn_id in range(3):
        rotated = jnp.einsum('ab,bqfe->aqfe', orient_mat[turn_id], gathered, precision=highest)
        turned = turned + jnp.where(rotation[None, None] == turn_id, rotated, 0.0)
    volume = jnp.zeros(own_part.shape, jnp.float32)
    for dim_id in range(3):
        inner_sum = jnp.einsum('bc,cqe->bqe', stiff_vol[dim_id], own_part, precision=highest)
        volume = volume + geometry[dim_id] * jnp.einsum('bqe,qr->bre', inner_sum, jacobians[dim_id], precision=highest)
    flux_sum = jnp.zeros(own_part.shape, jnp.float32)
    for face_id in range(4):
        local_term = jnp.einsum('cb,bqe->cqe', lifting[face_id], own_traces[:, :, face_id], precision=highest)
        neighbour_term = jnp.einsum('cb,bqe->cqe', lifting[face_id], turned[:, :, face_id], precision=highest)
        riemann = jnp.einsum('cqe,qr->cre', local_term, flux_minus[face_id], precision=highest)
        riemann = riemann + jnp.einsum('cqe,qr->cre', neighbour_term, flux_plus[face_id], precision=highest)
        flux_sum = flux_sum + geometry[3 + face_id] * riemann
    return volume - flux_sum


def global_partners(neighbour, send_elem):
    total_rows = neighbour.shape[1]
    element_ids = jnp.arange(total_rows, dtype=jnp.int32)
    device = element_ids // E_DEV
    is_ghost = neighbour >= E_DEV
    slot_all = jnp.maximum(neighbour - E_DEV, 0)
    direction = slot_all // SLOTS
    slot_id = slot_all % SLOTS
    offsets = jnp.array([-N_SUB, N_SUB, -1, 1], jnp.int32)
    source = jnp.clip(device[None, :] + offsets[direction], 0, N_DOM * N_SUB - 1)
    sent_elem = send_elem[direction, source * SLOTS + slot_id]
    return jnp.where(is_ghost, source * E_DEV + sent_elem, device[None, :] * E_DEV + neighbour).astype(jnp.int32)


def reference(solution, geometry, cluster, neighbour, orient, send_elem, stiff_time, stiff_vol, jacobians,
              flux_minus, flux_plus, lifting, restrict, orient_mat):
    partners = global_partners(neighbour, send_elem)
    first_part, late_part = predict(solution, geometry, stiff_time, jacobians,
                                    [(0.0, step_length), (step_length, 2.0 * step_length)])
    change_one = correct(first_part, first_part, partners, orient, geometry, stiff_vol, jacobians,
                         flux_minus, flux_plus, lifting, restrict, orient_mat)
    halfway = solution + change_one
    fine_part = predict(halfway, geometry, stiff_time, jacobians, [(0.0, step_length)])[0]
    second_part = jnp.where(cluster[None, None] == 0, fine_part, late_part)
    change_two = correct(second_part, second_part, partners, orient, geometry, stiff_vol, jacobians,
                         flux_minus, flux_plus, lifting, restrict, orient_mat)
    return halfway + change_two
```

```python
import functools
import jax
import jax.numpy as jnp
from jax import lax
from jax.experimental import pallas as pl
from jax.experimental.pallas import tpu as pltpu
from jax.sharding import PartitionSpec as P

STEP = 0.4
BASIS = 20
QUANT = 9
ROWS = 192
LANES = 256
TRACE = 96
ELEMS = 128
SLOTS = 32
MESH = pl.DeviceIdType.MESH
F32 = jnp.float32
BF16 = jnp.bfloat16


def nn(a, b):
    return lax.dot_general(a, b, (((1,), (0,)), ((), ())), preferred_element_type=F32)


def nt(a, b):
    return lax.dot_general(a, b, (((1,), (1,)), ((), ())), preferred_element_type=F32)


def exact(a, b):
    return lax.dot_general(
        a, b, (((1,), (0,)), ((), ())), precision=lax.Precision.HIGHEST, preferred_element_type=F32
    )


def split(x):
    hi = x.astype(BF16)
    return hi, (x - hi.astype(F32)).astype(BF16)


def wide(x):
    return jnp.concatenate(split(x), axis=1)


def tall(x):
    return jnp.concatenate(split(x), axis=0)


def onehot(mask):
    return jnp.where(mask, 1.0, 0.0).astype(BF16)


def iota(shape, dim):
    return lax.broadcasted_iota(jnp.int32, shape, dim)


def spread(x, places):
    hi, lo = split(x)
    return nn(hi, places) + nn(lo, places)


def lift_rows(rows, x):
    hi, lo = split(x)
    return nn(rows, hi) + nn(rows, lo)


def fold(product):
    half = product.shape[0] // 2
    top, bottom = product[:half], product[half:]
    return top[:, :ELEMS] + (top[:, ELEMS:] + bottom[:, :ELEMS])


def nine(index):
    return (index * 57) >> 9


def kernel(
    x_any, geo_any, clu_any, nb_any, ori_any, snd_any, st_any, sv_any, jac_any, fm_any, fp_any,
    lif_any, res_any, om_any, out_ref,
    x_in, geo_in, clu_in, nb_in, ori_in, snd_in, st_in, sv_in, jac_in, fm_in, fp_in, lif_in,
    res_in, om_in,
    x_ref, time_mat, vol_mat, own_mat, far_mat, trace_mat, near_hot, outgoing, ghosts,
    in_sem, send_sem, recv_sem,
):
    pairs = [
        (x_any, x_in), (st_any, st_in), (jac_any, jac_in), (geo_any, geo_in), (snd_any, snd_in),
        (res_any, res_in), (nb_any, nb_in), (ori_any, ori_in), (sv_any, sv_in), (fm_any, fm_in),
        (lif_any, lif_in), (om_any, om_in), (fp_any, fp_in), (clu_any, clu_in),
    ]
    loads = []
    for place, (source, target) in enumerate(pairs):
        load = pltpu.make_async_copy(source, target, in_sem.at[place])
        load.start()
        loads.append(load)

    dom, sub = lax.axis_index("dom"), lax.axis_index("sub")
    doms, subs = lax.axis_size("dom"), lax.axis_size("sub")
    dom_up, dom_down = lax.rem(dom + 1, doms), lax.rem(dom + doms - 1, doms)
    sub_up, sub_down = lax.rem(sub + 1, subs), lax.rem(sub + subs - 1, subs)
    targets = [(dom_up, sub), (dom_down, sub), (dom, sub_up), (dom, sub_down)]
    barrier = pltpu.get_barrier_semaphore()
    for target in targets:
        pl.semaphore_signal(barrier, inc=1, device_id=target, device_id_type=MESH)

    row = iota((ROWS, 32), 0)
    in_rows = row < BASIS * QUANT
    row_b = nine(row)
    row_q = row - QUANT * row_b
    basis_rows = onehot((row_b == iota((ROWS, 32), 1)) & in_rows)[:, :BASIS]
    quant_rows = onehot((row_q == iota((ROWS, 32), 1)) & in_rows)[:, :QUANT]
    col = iota((BASIS, LANES), 1)
    in_cols = col < BASIS * QUANT
    col_b = nine(col)
    col_q = col - QUANT * col_b
    basis_cols = onehot((col_b == iota((BASIS, LANES), 0)) & in_cols)
    quant_cols = onehot((col_q == iota((BASIS, LANES), 0)) & in_cols)[:QUANT]

    loads[1].wait()
    loads[2].wait()
    factors = jnp.concatenate([spread(jac_in[d].T, quant_cols) for d in range(3)], axis=1)
    jac_wide = lift_rows(quant_rows, factors)
    stiff = jnp.concatenate([spread(st_in[d], basis_cols) for d in range(3)], axis=1)
    time_mat[...] = tall(lift_rows(basis_rows, stiff) * jac_wide)

    loads[0].wait()
    for b in range(BASIS):
        x_ref[pl.ds(QUANT * b, QUANT), :] = x_in[b]
    x_ref[pl.ds(BASIS * QUANT, ROWS - BASIS * QUANT), :] = jnp.zeros(
        (ROWS - BASIS * QUANT, ELEMS), F32
    )
    loads[3].wait()
    blank = jnp.zeros((LANES - ROWS, 2 * ELEMS), BF16)

    def stacked(values, first, count):
        parts = []
        for g in range(first, first + count):
            parts += [wide(geo_in[pl.ds(g, 1), :] * values), blank]
        return jnp.concatenate(parts, axis=0)

    def predict(values, spans):
        current = values
        sums = [(b - a) * values for a, b in spans]
        factorial = 1.0
        for degree in range(1, 4):
            current = fold(nn(time_mat[...], stacked(current, 0, 3)))
            factorial = factorial * (degree + 1)
            sign = -1.0 if degree % 2 else 1.0
            sums = [
                s + (sign * (b ** (degree + 1) - a ** (degree + 1)) / factorial) * current
                for s, (a, b) in zip(sums, spans)
            ]
        return sums

    first_part, late_part = predict(x_ref[...], [(0.0, STEP), (STEP, 2.0 * STEP)])

    loads[4].wait()
    eye = onehot(iota((SLOTS, SLOTS), 0) == iota((SLOTS, SLOTS), 1))
    named = nt(eye, snd_in[...].astype(F32).astype(BF16))
    elem = iota((SLOTS, ELEMS), 1)
    picks = jnp.concatenate(
        [onehot(named[:, d : d + 1].astype(jnp.int32) == elem) for d in range(4)], axis=0
    )
    pick_both = jnp.concatenate([picks, picks], axis=1)

    def send(turn, values):
        outgoing[turn, :, pl.ds(0, ROWS)] = nt(pick_both, wide(values))
        if turn == 0:
            pl.semaphore_wait(barrier, 4)
        copies = []
        for d in range(4):
            part = pl.ds(SLOTS * d, SLOTS)
            copy = pltpu.make_async_remote_copy(
                src_ref=outgoing.at[turn, part],
                dst_ref=ghosts.at[turn, part],
                send_sem=send_sem.at[turn, d],
                recv_sem=recv_sem.at[turn, d],
                device_id=targets[d],
                device_id_type=MESH,
            )
            copy.start()
            copies.append(copy)
        return copies

    copies_one = send(0, first_part)

    loads[5].wait()
    face_row = iota((TRACE, 16), 0)
    face_b = nine(face_row)
    face_rows = onehot((face_b == iota((TRACE, 16), 1)) & (face_row < 90))[:, :10]
    same_row = iota((TRACE, ROWS), 0)
    same_col = iota((TRACE, ROWS), 1)
    same = (same_row - QUANT * nine(same_row)) == (same_col - QUANT * nine(same_col))
    trace_blocks = []
    for j in range(4):
        block = lift_rows(face_rows, spread(res_in[j], basis_cols[:, :ROWS]))
        trace_blocks.append(jnp.where(same, block, 0.0))
    trace_mat[...] = tall(jnp.concatenate(trace_blocks, axis=0))

    loads[6].wait()
    loads[7].wait()
    facing = (ori_in[...] * 11) >> 5
    turning = ori_in[...] - 3 * facing
    behind = nb_in[...]
    near_key = jnp.where(behind < ELEMS, behind + ELEMS * facing, -1)
    key_row = iota((4 * ELEMS, ELEMS), 0)
    for f in range(4):
        near_hot[:, pl.ds(ELEMS * f, ELEMS)] = onehot(key_row == near_key[f : f + 1])

    slot_row = iota((ELEMS, ELEMS), 0) + ELEMS
    info_row = iota((16, ELEMS), 0)
    slot_info = jnp.zeros((16, ELEMS), F32)
    slot_hot = jnp.zeros((ELEMS, ELEMS), F32)
    for f in range(4):
        hot = jnp.where(slot_row == behind[f : f + 1], 1.0, 0.0)
        slot_hot = slot_hot + hot
        scale = geo_in[pl.ds(3 + f, 1), :]
        scale_hi = scale.astype(BF16).astype(F32)
        scale_mid = (scale - scale_hi).astype(BF16).astype(F32)
        scale_low = scale - scale_hi - scale_mid
        info = jnp.where(info_row == 0, facing[f : f + 1].astype(F32), 0.0)
        info = jnp.where(info_row == 1, (4 * turning[f : f + 1] + f).astype(F32), info)
        info = jnp.where(info_row == 2, scale_hi, info)
        info = jnp.where(info_row == 3, scale_mid, info)
        info = jnp.where(info_row == 4, scale_low, info)
        slot_info = slot_info + nt(info.astype(BF16), hot.astype(BF16))
    slot_hot = slot_hot.astype(BF16)
    slot_both = jnp.concatenate([slot_hot, slot_hot], axis=0)
    slot_face = slot_info[0:1]
    slot_kind = slot_info[1:2]
    slot_scale = slot_info[2:3] + slot_info[3:4] + slot_info[4:5]

    def mask_of(lanes):
        piece = jnp.broadcast_to(jnp.where(lanes, 1.0, 0.0), (16, ELEMS)).astype(BF16)
        piece = jnp.concatenate([piece] * (TRACE // 16), axis=0)
        return jnp.concatenate([piece, piece], axis=1)

    loads[8].wait()
    stiff = jnp.concatenate([spread(sv_in[d], basis_cols) for d in range(3)], axis=1)
    vol_mat[...] = tall(lift_rows(basis_rows, stiff) * jac_wide)
    loads[9].wait()
    loads[10].wait()
    fluxes = jnp.concatenate([spread(-fm_in[f].T, quant_cols) for f in range(4)], axis=1)
    lifted = jnp.concatenate(
        [spread(exact(lif_in[f], res_in[f]), basis_cols) for f in range(4)], axis=1
    )
    own_mat[...] = tall(lift_rows(basis_rows, lifted) * lift_rows(quant_rows, fluxes))

    loads[11].wait()
    loads[12].wait()
    far_col = iota((16, 4 * TRACE), 1)
    far_face = (far_col * 683) >> 16
    far_rem = far_col - TRACE * far_face
    far_b = nine(far_rem)
    far_q = far_rem - QUANT * far_b
    far_in = far_rem < 90
    far_row = iota((16, 4 * TRACE), 0)
    far_basis = (far_b == far_row) & far_in
    far_basis_hot = onehot(far_basis)[:10]
    lifted_far = []
    for h in range(3):
        turned = spread(om_in[h], far_basis_hot)
        total = jnp.zeros((BASIS, 4 * TRACE), F32)
        for f in range(4):
            hi, lo = split(jnp.where(far_face[:10] == f, turned, 0.0))
            lift_hi, lift_lo = split(lif_in[f])
            total = total + (nn(lift_hi, hi) + nn(lift_hi, lo) + nn(lift_lo, hi))
        lifted_far.append(total)
    lifted_far = jnp.concatenate(lifted_far, axis=1)
    flux_far = jnp.zeros((QUANT, 4 * TRACE), F32)
    for f in range(4):
        places = onehot((far_q == far_row) & far_in & (far_face == f))[:QUANT]
        flux_far = flux_far + spread(-fp_in[f].T, places)
    flux_far = lift_rows(quant_rows, flux_far)
    flux_far = jnp.concatenate([flux_far] * 3, axis=1)
    far_mat[...] = tall(lift_rows(basis_rows, lifted_far) * flux_far)

    near_masks = [[mask_of(turning[f : f + 1] == h) for f in range(4)] for h in range(3)]
    slot_masks = [[mask_of(slot_kind == 4.0 * h + f) for f in range(4)] for h in range(3)]

    def correct_near(values):
        change = fold(nn(vol_mat[...], stacked(values, 0, 3)))
        change = change + fold(nn(own_mat[...], stacked(values, 3, 4)))
        traces = fold(nn(trace_mat[...], wide(values)))
        sources = jnp.concatenate(
            [traces[TRACE * j : TRACE * (j + 1)] for j in range(4)], axis=1
        )
        picked = nn(tall(sources), near_hot[...])
        picked = picked[:TRACE] + picked[TRACE:]
        scaled = [
            wide(geo_in[pl.ds(3 + f, 1), :] * picked[:, ELEMS * f : ELEMS * (f + 1)])
            for f in range(4)
        ]
        parts = [scaled[f] * near_masks[h][f] for h in range(3) for f in range(4)]
        return change + fold(nn(far_mat[...], jnp.concatenate(parts, axis=0)))

    def correct_far(turn):
        slots = ghosts[turn, :, pl.ds(0, ROWS)]
        traces = fold(nt(trace_mat[...], tall(slots)))
        chosen = traces[:TRACE]
        for j in range(1, 4):
            chosen = jnp.where(slot_face == j, traces[TRACE * j : TRACE * (j + 1)], chosen)
        scaled = wide(slot_scale * chosen)
        parts = [scaled * slot_masks[h][f] for h in range(3) for f in range(4)]
        lifted = fold(nn(far_mat[...], jnp.concatenate(parts, axis=0)))
        return nn(wide(lifted), slot_both)

    def finish(copies):
        for copy in copies:
            copy.wait_recv()

    near_one = x_ref[...] + correct_near(first_part)
    finish(copies_one)
    halfway = near_one + correct_far(0)
    fine_part = predict(halfway, [(0.0, STEP)])[0]
    loads[13].wait()
    second_part = jnp.where(clu_in[...] == 0, fine_part, late_part)
    copies_two = send(1, second_part)
    near_two = halfway + correct_near(second_part)
    finish(copies_two)
    out_ref[...] = (near_two + correct_far(1))[: BASIS * QUANT]
    for copy in copies_one + copies_two:
        copy.wait_send()


def local(solution, geometry, cluster, *others):
    args = (solution, geometry, cluster.reshape(1, ELEMS), *others)
    held = [pltpu.VMEM(a.shape, a.dtype) for a in args]
    result = pl.pallas_call(
        kernel,
        out_shape=jax.ShapeDtypeStruct((BASIS * QUANT, ELEMS), F32),
        in_specs=[pl.BlockSpec(memory_space=pl.ANY)] * len(args),
        out_specs=pl.BlockSpec(memory_space=pltpu.VMEM),
        scratch_shapes=held
        + [
            pltpu.VMEM((ROWS, ELEMS), F32),
            pltpu.VMEM((2 * ROWS, 3 * LANES), BF16),
            pltpu.VMEM((2 * ROWS, 3 * LANES), BF16),
            pltpu.VMEM((2 * ROWS, 4 * LANES), BF16),
            pltpu.VMEM((2 * ROWS, 12 * TRACE), BF16),
            pltpu.VMEM((8 * TRACE, ROWS), BF16),
            pltpu.VMEM((4 * ELEMS, 4 * ELEMS), BF16),
            pltpu.VMEM((2, ELEMS, LANES), F32),
            pltpu.VMEM((2, ELEMS, LANES), F32),
            pltpu.SemaphoreType.DMA((len(args),)),
            pltpu.SemaphoreType.DMA((2, 4)),
            pltpu.SemaphoreType.DMA((2, 4)),
        ],
        compiler_params=pltpu.CompilerParams(
            collective_id=0, has_side_effects=True, vmem_limit_bytes=32 * 1024 * 1024
        ),
    )(*args)
    return result.reshape(solution.shape)


def solution(mesh):
    split_last = P(None, ("dom", "sub"))
    return jax.shard_map(
        local,
        mesh=mesh,
        in_specs=(P(None, None, ("dom", "sub")), split_last, P(("dom", "sub")))
        + (split_last,) * 3
        + (P(),) * 8,
        out_specs=P(None, None, ("dom", "sub")),
        check_vma=False,
    )
```

```python
import functools
import jax
import jax.numpy as jnp
from jax import lax
from jax.experimental import pallas as pl
from jax.experimental.pallas import tpu as pltpu
from jax.sharding import PartitionSpec as P

STEP = 0.4
BASIS = 20
QUANT = 9
ROWS = 192
LANES = 256
TRACE = 96
ELEMS = 128
SLOTS = 32
MESH = pl.DeviceIdType.MESH
F32 = jnp.float32
BF16 = jnp.bfloat16


def nn(a, b):
    return lax.dot_general(a, b, (((1,), (0,)), ((), ())), preferred_element_type=F32)


def nt(a, b):
    return lax.dot_general(a, b, (((1,), (1,)), ((), ())), preferred_element_type=F32)


def exact(a, b):
    return lax.dot_general(
        a, b, (((1,), (0,)), ((), ())), precision=lax.Precision.HIGHEST, preferred_element_type=F32
    )


def split(x):
    hi = x.astype(BF16)
    return hi, (x - hi.astype(F32)).astype(BF16)


def wide(x):
    return jnp.concatenate(split(x), axis=1)


def tall(x):
    return jnp.concatenate(split(x), axis=0)


def onehot(mask):
    return jnp.where(mask, 1.0, 0.0).astype(BF16)


def iota(shape, dim):
    return lax.broadcasted_iota(jnp.int32, shape, dim)


def spread(x, places):
    hi, lo = split(x)
    return nn(hi, places) + nn(lo, places)


def lift_rows(rows, x):
    hi, lo = split(x)
    return nn(rows, hi) + nn(rows, lo)


def fold(product):
    half = product.shape[0] // 2
    top, bottom = product[:half], product[half:]
    return top[:, :ELEMS] + (top[:, ELEMS:] + bottom[:, :ELEMS])


def by_basis(index):
    return (index * 205) >> 12


def by_face_basis(index):
    return (index * 205) >> 11


def kernel(
    x_any, geo_any, clu_any, nb_any, ori_any, snd_any, st_any, sv_any, jac_any, fm_any, fp_any,
    lif_any, res_any, om_any, out_ref,
    x_in, geo_in, clu_in, nb_in, ori_in, snd_in, st_in, sv_in, jac_in, fm_in, fp_in, lif_in,
    res_in, om_in,
    x_ref, time_mat, vol_mat, own_mat, far_mat, trace_mat, near_hot, outgoing, ghosts,
    in_sem, send_sem, recv_sem,
):
    pairs = [
        (x_any, x_in), (st_any, st_in), (jac_any, jac_in), (geo_any, geo_in), (snd_any, snd_in),
        (res_any, res_in), (nb_any, nb_in), (ori_any, ori_in), (sv_any, sv_in), (fm_any, fm_in),
        (lif_any, lif_in), (om_any, om_in), (fp_any, fp_in), (clu_any, clu_in),
    ]
    loads = []
    for place, (source, target) in enumerate(pairs):
        load = pltpu.make_async_copy(source, target, in_sem.at[place])
        load.start()
        loads.append(load)

    dom, sub = lax.axis_index("dom"), lax.axis_index("sub")
    doms, subs = lax.axis_size("dom"), lax.axis_size("sub")
    dom_up, dom_down = lax.rem(dom + 1, doms), lax.rem(dom + doms - 1, doms)
    sub_up, sub_down = lax.rem(sub + 1, subs), lax.rem(sub + subs - 1, subs)
    targets = [(dom_up, sub), (dom_down, sub), (dom, sub_up), (dom, sub_down)]
    barrier = pltpu.get_barrier_semaphore()
    for target in targets:
        pl.semaphore_signal(barrier, inc=1, device_id=target, device_id_type=MESH)

    row = iota((ROWS, 32), 0)
    in_rows = row < BASIS * QUANT
    row_q = by_basis(row)
    row_b = row - BASIS * row_q
    basis_rows = onehot((row_b == iota((ROWS, 32), 1)) & in_rows)[:, :BASIS]
    quant_rows = onehot((row_q == iota((ROWS, 32), 1)) & in_rows)[:, :QUANT]
    col = iota((BASIS, LANES), 1)
    in_cols = col < BASIS * QUANT
    col_q = by_basis(col)
    col_b = col - BASIS * col_q
    basis_cols = onehot((col_b == iota((BASIS, LANES), 0)) & in_cols)
    quant_cols = onehot((col_q == iota((BASIS, LANES), 0)) & in_cols)[:QUANT]

    loads[1].wait()
    loads[2].wait()
    factors = jnp.concatenate([spread(jac_in[:, d, :].T, quant_cols) for d in range(3)], axis=1)
    jac_wide = lift_rows(quant_rows, factors)
    stiff = jnp.concatenate([spread(st_in[d], basis_cols) for d in range(3)], axis=1)
    time_mat[...] = tall(lift_rows(basis_rows, stiff) * jac_wide)

    loads[0].wait()
    for q in range(QUANT):
        x_ref[pl.ds(BASIS * q, BASIS), :] = x_in[q]
    x_ref[pl.ds(BASIS * QUANT, ROWS - BASIS * QUANT), :] = jnp.zeros(
        (ROWS - BASIS * QUANT, ELEMS), F32
    )
    loads[3].wait()
    blank = jnp.zeros((LANES - ROWS, 2 * ELEMS), BF16)

    def stacked(values, first, count):
        parts = []
        for g in range(first, first + count):
            parts += [wide(geo_in[pl.ds(g, 1), :] * values), blank]
        return jnp.concatenate(parts, axis=0)

    def predict(values, spans):
        current = values
        sums = [(b - a) * values for a, b in spans]
        factorial = 1.0
        for degree in range(1, 4):
            current = fold(nn(time_mat[...], stacked(current, 0, 3)))
            factorial = factorial * (degree + 1)
            sign = -1.0 if degree % 2 else 1.0
            sums = [
                s + (sign * (b ** (degree + 1) - a ** (degree + 1)) / factorial) * current
                for s, (a, b) in zip(sums, spans)
            ]
        return sums

    first_part, late_part = predict(x_ref[...], [(0.0, STEP), (STEP, 2.0 * STEP)])

    loads[4].wait()
    eye = onehot(iota((SLOTS, SLOTS), 0) == iota((SLOTS, SLOTS), 1))
    named = nt(eye, snd_in[...].astype(F32).astype(BF16))
    elem = iota((SLOTS, ELEMS), 1)
    picks = jnp.concatenate(
        [onehot(named[:, d : d + 1].astype(jnp.int32) == elem) for d in range(4)], axis=0
    )
    pick_both = jnp.concatenate([picks, picks], axis=1)

    def send(turn, values):
        outgoing[turn, :, pl.ds(0, ROWS)] = nt(pick_both, wide(values))
        if turn == 0:
            pl.semaphore_wait(barrier, 4)
        copies = []
        for d in range(4):
            part = pl.ds(SLOTS * d, SLOTS)
            copy = pltpu.make_async_remote_copy(
                src_ref=outgoing.at[turn, part],
                dst_ref=ghosts.at[turn, part],
                send_sem=send_sem.at[turn, d],
                recv_sem=recv_sem.at[turn, d],
                device_id=targets[d],
                device_id_type=MESH,
            )
            copy.start()
            copies.append(copy)
        return copies

    copies_one = send(0, first_part)

    loads[5].wait()
    face_row = iota((TRACE, 16), 0)
    face_b = face_row - 10 * by_face_basis(face_row)
    face_rows = onehot((face_b == iota((TRACE, 16), 1)) & (face_row < 90))[:, :10]
    same_row = iota((TRACE, ROWS), 0)
    same_col = iota((TRACE, ROWS), 1)
    same = by_face_basis(same_row) == by_basis(same_col)
    trace_blocks = []
    for j in range(4):
        block = lift_rows(face_rows, spread(res_in[:, j, :], basis_cols[:, :ROWS]))
        trace_blocks.append(jnp.where(same, block, 0.0))
    trace_mat[...] = tall(jnp.concatenate(trace_blocks, axis=0))

    loads[6].wait()
    loads[7].wait()
    facing = (ori_in[...] * 11) >> 5
    turning = ori_in[...] - 3 * facing
    behind = nb_in[...]
    near_key = jnp.where(behind < ELEMS, behind + ELEMS * facing, -1)
    key_row = iota((4 * ELEMS, ELEMS), 0)
    for f in range(4):
        near_hot[:, pl.ds(ELEMS * f, ELEMS)] = onehot(key_row == near_key[f : f + 1])

    slot_row = iota((ELEMS, ELEMS), 0) + ELEMS
    info_row = iota((16, ELEMS), 0)
    slot_info = jnp.zeros((16, ELEMS), F32)
    slot_hot = jnp.zeros((ELEMS, ELEMS), F32)
    for f in range(4):
        hot = jnp.where(slot_row == behind[f : f + 1], 1.0, 0.0)
        slot_hot = slot_hot + hot
        scale = geo_in[pl.ds(3 + f, 1), :]
        scale_hi = scale.astype(BF16).astype(F32)
        scale_mid = (scale - scale_hi).astype(BF16).astype(F32)
        scale_low = scale - scale_hi - scale_mid
        info = jnp.where(info_row == 0, facing[f : f + 1].astype(F32), 0.0)
        info = jnp.where(info_row == 1, (4 * turning[f : f + 1] + f).astype(F32), info)
        info = jnp.where(info_row == 2, scale_hi, info)
        info = jnp.where(info_row == 3, scale_mid, info)
        info = jnp.where(info_row == 4, scale_low, info)
        slot_info = slot_info + nt(info.astype(BF16), hot.astype(BF16))
    slot_hot = slot_hot.astype(BF16)
    slot_both = jnp.concatenate([slot_hot, slot_hot], axis=0)
    slot_face = slot_info[0:1]
    slot_kind = slot_info[1:2]
    slot_scale = slot_info[2:3] + slot_info[3:4] + slot_info[4:5]

    def mask_of(lanes):
        piece = jnp.broadcast_to(jnp.where(lanes, 1.0, 0.0), (16, ELEMS)).astype(BF16)
        piece = jnp.concatenate([piece] * (TRACE // 16), axis=0)
        return jnp.concatenate([piece, piece], axis=1)

    loads[8].wait()
    stiff = jnp.concatenate([spread(sv_in[d], basis_cols) for d in range(3)], axis=1)
    vol_mat[...] = tall(lift_rows(basis_rows, stiff) * jac_wide)
    loads[9].wait()
    loads[10].wait()
    fluxes = jnp.concatenate([spread(-fm_in[:, f, :].T, quant_cols) for f in range(4)], axis=1)
    lifted = jnp.concatenate(
        [spread(exact(lif_in[:, f, :].T, res_in[:, f, :]), basis_cols) for f in range(4)], axis=1
    )
    own_mat[...] = tall(lift_rows(basis_rows, lifted) * lift_rows(quant_rows, fluxes))

    loads[11].wait()
    loads[12].wait()
    far_col = iota((16, 4 * TRACE), 1)
    far_face = (far_col * 683) >> 16
    far_rem = far_col - TRACE * far_face
    far_q = by_face_basis(far_rem)
    far_b = far_rem - 10 * far_q
    far_in = far_rem < 90
    far_row = iota((16, 4 * TRACE), 0)
    far_basis = (far_b == far_row) & far_in
    far_basis_hot = onehot(far_basis)[:10]
    lifted_far = []
    for h in range(3):
        turned = spread(om_in[:, h, :], far_basis_hot)
        total = jnp.zeros((BASIS, 4 * TRACE), F32)
        for f in range(4):
            hi, lo = split(jnp.where(far_face[:10] == f, turned, 0.0))
            lift_hi, lift_lo = split(lif_in[:, f, :].T)
            total = total + (nn(lift_hi, hi) + nn(lift_hi, lo) + nn(lift_lo, hi))
        lifted_far.append(total)
    lifted_far = jnp.concatenate(lifted_far, axis=1)
    flux_far = jnp.zeros((QUANT, 4 * TRACE), F32)
    for f in range(4):
        places = onehot((far_q == far_row) & far_in & (far_face == f))[:QUANT]
        flux_far = flux_far + spread(-fp_in[:, f, :].T, places)
    flux_far = lift_rows(quant_rows, flux_far)
    flux_far = jnp.concatenate([flux_far] * 3, axis=1)
    far_mat[...] = tall(lift_rows(basis_rows, lifted_far) * flux_far)

    near_masks = [[mask_of(turning[f : f + 1] == h) for f in range(4)] for h in range(3)]
    slot_masks = [[mask_of(slot_kind == 4.0 * h + f) for f in range(4)] for h in range(3)]

    def correct_near(values):
        change = fold(nn(vol_mat[...], stacked(values, 0, 3)))
        change = change + fold(nn(own_mat[...], stacked(values, 3, 4)))
        traces = fold(nn(trace_mat[...], wide(values)))
        sources = jnp.concatenate(
            [traces[TRACE * j : TRACE * (j + 1)] for j in range(4)], axis=1
        )
        picked = nn(tall(sources), near_hot[...])
        picked = picked[:TRACE] + picked[TRACE:]
        scaled = [
            wide(geo_in[pl.ds(3 + f, 1), :] * picked[:, ELEMS * f : ELEMS * (f + 1)])
            for f in range(4)
        ]
        parts = [scaled[f] * near_masks[h][f] for h in range(3) for f in range(4)]
        return change + fold(nn(far_mat[...], jnp.concatenate(parts, axis=0)))

    def correct_far(turn):
        slots = ghosts[turn, :, pl.ds(0, ROWS)]
        traces = fold(nt(trace_mat[...], tall(slots)))
        chosen = traces[:TRACE]
        for j in range(1, 4):
            chosen = jnp.where(slot_face == j, traces[TRACE * j : TRACE * (j + 1)], chosen)
        scaled = wide(slot_scale * chosen)
        parts = [scaled * slot_masks[h][f] for h in range(3) for f in range(4)]
        lifted = fold(nn(far_mat[...], jnp.concatenate(parts, axis=0)))
        return nn(wide(lifted), slot_both)

    def finish(copies):
        for copy in copies:
            copy.wait_recv()

    near_one = x_ref[...] + correct_near(first_part)
    finish(copies_one)
    halfway = near_one + correct_far(0)
    fine_part = predict(halfway, [(0.0, STEP)])[0]
    loads[13].wait()
    second_part = jnp.where(clu_in[...] == 0, fine_part, late_part)
    copies_two = send(1, second_part)
    near_two = halfway + correct_near(second_part)
    finish(copies_two)
    x_ref[...] = near_two + correct_far(1)
    for q in range(QUANT):
        out_ref[q] = x_ref[pl.ds(BASIS * q, BASIS), :]
    for copy in copies_one + copies_two:
        copy.wait_send()


def local(
    solution, geometry, cluster, neighbour, orient, send_elem, stiff_time, stiff_vol, jacobians,
    flux_minus, flux_plus, lifting, restrict, orient_mat,
):
    inner = (1, 0, 2)
    args = (
        solution.transpose(inner), geometry, cluster.reshape(1, ELEMS), neighbour, orient,
        send_elem, stiff_time, stiff_vol, jacobians.transpose(inner),
        flux_minus.transpose(inner), flux_plus.transpose(inner), lifting.transpose(2, 0, 1),
        restrict.transpose(inner), orient_mat.transpose(inner),
    )
    held = [pltpu.VMEM(a.shape, a.dtype) for a in args]
    result = pl.pallas_call(
        kernel,
        out_shape=jax.ShapeDtypeStruct((QUANT, BASIS, ELEMS), F32),
        in_specs=[pl.BlockSpec(memory_space=pl.ANY)] * len(args),
        out_specs=pl.BlockSpec(memory_space=pltpu.VMEM),
        scratch_shapes=held
        + [
            pltpu.VMEM((ROWS, ELEMS), F32),
            pltpu.VMEM((2 * ROWS, 3 * LANES), BF16),
            pltpu.VMEM((2 * ROWS, 3 * LANES), BF16),
            pltpu.VMEM((2 * ROWS, 4 * LANES), BF16),
            pltpu.VMEM((2 * ROWS, 12 * TRACE), BF16),
            pltpu.VMEM((8 * TRACE, ROWS), BF16),
            pltpu.VMEM((4 * ELEMS, 4 * ELEMS), BF16),
            pltpu.VMEM((2, ELEMS, LANES), F32),
            pltpu.VMEM((2, ELEMS, LANES), F32),
            pltpu.SemaphoreType.DMA((len(args),)),
            pltpu.SemaphoreType.DMA((2, 4)),
            pltpu.SemaphoreType.DMA((2, 4)),
        ],
        compiler_params=pltpu.CompilerParams(
            collective_id=0, has_side_effects=True, vmem_limit_bytes=60 * 1024 * 1024
        ),
    )(*args)
    return result.transpose(inner)


def solution(mesh):
    split_last = P(None, ("dom", "sub"))
    return jax.shard_map(
        local,
        mesh=mesh,
        in_specs=(P(None, None, ("dom", "sub")), split_last, P(("dom", "sub")))
        + (split_last,) * 3
        + (P(),) * 8,
        out_specs=P(None, None, ("dom", "sub")),
        check_vma=False,
    )
```

```python
import functools
import jax
import jax.numpy as jnp
from jax import lax
from jax.experimental import pallas as pl
from jax.experimental.pallas import tpu as pltpu
from jax.sharding import PartitionSpec as P

STEP = 0.4
BASIS = 20
QUANT = 9
ROWS = 192
LANES = 256
TRACE = 96
ELEMS = 128
SLOTS = 32
MESH = pl.DeviceIdType.MESH
F32 = jnp.float32
BF16 = jnp.bfloat16


def nn(a, b):
    return lax.dot_general(a, b, (((1,), (0,)), ((), ())), preferred_element_type=F32)


def nt(a, b):
    return lax.dot_general(a, b, (((1,), (1,)), ((), ())), preferred_element_type=F32)


def split(x):
    hi = x.astype(BF16)
    return hi, (x - hi.astype(F32)).astype(BF16)


def wide(x):
    return jnp.concatenate(split(x), axis=1)


def tall(x):
    return jnp.concatenate(split(x), axis=0)


def onehot(mask):
    return jnp.where(mask, 1.0, 0.0).astype(BF16)


def iota(shape, dim):
    return lax.broadcasted_iota(jnp.int32, shape, dim)


def triple(x):
    hi, lo = split(x)
    return jnp.concatenate([hi, lo, hi], axis=1)


def stack(pairs):
    his = [hi for hi, _ in pairs]
    return jnp.concatenate(his + his + [lo for _, lo in pairs], axis=0)


def spread(x, places):
    hi, lo = split(x)
    return nn(hi, places) + nn(lo, places)


def triple_product(x, y):
    x_hi, x_lo = split(x)
    y_hi, y_lo = split(y)
    return nn(x_hi, y_hi) + (nn(x_hi, y_lo) + nn(x_lo, y_hi))


def kron(held, left, right):
    wide_part = pl.ds(0, left.shape[1])
    for q in range(QUANT):
        held[pl.ds(BASIS * q, BASIS), wide_part] = left * right[q : q + 1]
    held[pl.ds(BASIS * QUANT, ROWS - BASIS * QUANT), wide_part] = jnp.zeros(
        (ROWS - BASIS * QUANT, left.shape[1]), F32
    )
    return held[:, wide_part]


def by_basis(index):
    return (index * 205) >> 12


def by_face_basis(index):
    return (index * 205) >> 11


def kernel(
    x_any, geo_any, clu_any, nb_any, ori_any, snd_any, st_any, sv_any, jac_any, fm_any, fp_any,
    lif_any, res_any, om_any, out_ref,
    x_in, geo_in, clu_in, nb_in, ori_in, snd_in, st_in, sv_in, jac_in, fm_in, fp_in, lif_in,
    res_in, om_in,
    x_ref, time_held, vol_held, own_held, far_held, trace_held, time_mat, vol_mat, own_mat, far_mat,
    trace_mat, near_hot, ghost_hot, outgoing, ghosts,
    in_sem, send_sem, recv_sem,
):
    pairs = [
        (x_any, x_in), (st_any, st_in), (jac_any, jac_in), (geo_any, geo_in), (snd_any, snd_in),
        (res_any, res_in), (nb_any, nb_in), (ori_any, ori_in), (sv_any, sv_in), (fm_any, fm_in),
        (lif_any, lif_in), (om_any, om_in), (fp_any, fp_in), (clu_any, clu_in),
    ]
    loads = []
    for place, (source, target) in enumerate(pairs):
        load = pltpu.make_async_copy(source, target, in_sem.at[place])
        load.start()
        loads.append(load)

    dom, sub = lax.axis_index("dom"), lax.axis_index("sub")
    doms, subs = lax.axis_size("dom"), lax.axis_size("sub")
    dom_up, dom_down = lax.rem(dom + 1, doms), lax.rem(dom + doms - 1, doms)
    sub_up, sub_down = lax.rem(sub + 1, subs), lax.rem(sub + subs - 1, subs)
    targets = [(dom_up, sub), (dom_down, sub), (dom, sub_up), (dom, sub_down)]
    barrier = pltpu.get_barrier_semaphore()
    for target in targets:
        pl.semaphore_signal(barrier, inc=1, device_id=target, device_id_type=MESH)

    col = iota((BASIS, ROWS), 1)
    in_cols = col < BASIS * QUANT
    col_q = by_basis(col)
    col_b = col - BASIS * col_q
    basis_cols = onehot((col_b == iota((BASIS, ROWS), 0)) & in_cols)
    quant_cols = onehot((col_q == iota((BASIS, ROWS), 0)) & in_cols)[:QUANT]

    loads[1].wait()
    loads[2].wait()
    factors = jnp.concatenate([spread(jac_in[:, d, :].T, quant_cols) for d in range(3)], axis=1)
    stiff = jnp.concatenate([spread(st_in[d], basis_cols) for d in range(3)], axis=1)
    time_mat[...] = triple(kron(time_held, stiff, factors))

    loads[0].wait()
    for q in range(QUANT):
        x_ref[pl.ds(BASIS * q, BASIS), :] = x_in[q]
    x_ref[pl.ds(BASIS * QUANT, ROWS - BASIS * QUANT), :] = jnp.zeros(
        (ROWS - BASIS * QUANT, ELEMS), F32
    )
    loads[3].wait()

    def scaled_three(values):
        return stack([split(geo_in[pl.ds(g, 1), :] * values) for g in range(3)])

    def predict(values, spans):
        current = values
        sums = [(b - a) * values for a, b in spans]
        factorial = 1.0
        for degree in range(1, 4):
            current = nn(time_mat[...], scaled_three(current))
            factorial = factorial * (degree + 1)
            sign = -1.0 if degree % 2 else 1.0
            sums = [
                s + (sign * (b ** (degree + 1) - a ** (degree + 1)) / factorial) * current
                for s, (a, b) in zip(sums, spans)
            ]
        return sums

    first_part, late_part = predict(x_ref[...], [(0.0, STEP), (STEP, 2.0 * STEP)])

    loads[4].wait()
    eye = onehot(iota((SLOTS, SLOTS), 0) == iota((SLOTS, SLOTS), 1))
    named = nt(eye, snd_in[...].astype(F32).astype(BF16))
    elem = iota((SLOTS, ELEMS), 1)
    picks = jnp.concatenate(
        [onehot(named[:, d : d + 1].astype(jnp.int32) == elem) for d in range(4)], axis=0
    )
    pick_both = jnp.concatenate([picks, picks], axis=1)

    outgoing[:, :, pl.ds(ROWS, LANES - ROWS)] = jnp.zeros((2, ELEMS, LANES - ROWS), F32)

    def send(turn, values):
        outgoing[turn, :, pl.ds(0, ROWS)] = nt(pick_both, wide(values))
        if turn == 0:
            pl.semaphore_wait(barrier, 4)
        copies = []
        for d in range(4):
            part = pl.ds(SLOTS * d, SLOTS)
            copy = pltpu.make_async_remote_copy(
                src_ref=outgoing.at[turn, part],
                dst_ref=ghosts.at[turn, part],
                send_sem=send_sem.at[turn, d],
                recv_sem=recv_sem.at[turn, d],
                device_id=targets[d],
                device_id_type=MESH,
            )
            copy.start()
            copies.append(copy)
        return copies

    copies_one = send(0, first_part)

    loads[5].wait()
    trace_col = iota((10, LANES), 1)
    trace_q = by_basis(trace_col)
    for j in range(4):
        places = onehot(
            (iota((BASIS, LANES), 1) - BASIS * by_basis(iota((BASIS, LANES), 1)))
            == iota((BASIS, LANES), 0)
        )
        block = spread(res_in[:, j, :], places)
        for q in range(QUANT):
            trace_held[pl.ds(TRACE * j + 10 * q, 10), :] = jnp.where(trace_q == q, block, 0.0)
        trace_held[pl.ds(TRACE * j + 90, TRACE - 90), :] = jnp.zeros((TRACE - 90, LANES), F32)
    trace_mat[...] = triple(trace_held[...])

    loads[6].wait()
    loads[7].wait()
    facing = (ori_in[...] * 11) >> 5
    turning = ori_in[...] - 3 * facing
    behind = nb_in[...]
    near_key = jnp.where(behind < ELEMS, behind + ELEMS * facing, -1)
    key_row = iota((4 * ELEMS, ELEMS), 0)
    slot_row = iota((ELEMS, ELEMS), 0) + ELEMS
    slot_face = jnp.zeros((16, ELEMS), F32)
    for f in range(4):
        part = pl.ds(ELEMS * f, ELEMS)
        near_hot[:, part] = onehot(key_row == near_key[f : f + 1])
        hot = onehot(slot_row == behind[f : f + 1])
        ghost_hot[:, part] = hot
        face = jnp.broadcast_to(facing[f : f + 1].astype(F32), (16, ELEMS)).astype(BF16)
        slot_face = slot_face + nt(face, hot)
    slot_face = slot_face[0:1]

    loads[8].wait()
    stiff = jnp.concatenate([spread(sv_in[d], basis_cols) for d in range(3)], axis=1)
    vol_mat[...] = triple(kron(vol_held, stiff, factors))

    loads[9].wait()
    loads[10].wait()
    loads[11].wait()
    loads[12].wait()
    far_col = iota((16, TRACE), 1)
    far_q = by_face_basis(far_col)
    far_row = iota((16, TRACE), 0)
    far_in = far_col < 90
    far_basis = onehot((far_col - 10 * far_q == far_row) & far_in)[:10]
    far_quant = onehot((far_q == far_row) & far_in)[:QUANT]
    turned = jnp.concatenate([spread(om_in[:, h, :], far_basis) for h in range(3)], axis=1)
    own_left, own_right, far_left, far_right = [], [], [], []
    for f in range(4):
        lifting = lif_in[:, f, :].T
        own_left.append(spread(lifting, far_basis))
        own_right.append(spread(-fm_in[:, f, :].T, far_quant))
        far_left.append(triple_product(lifting, turned))
        far_right += [spread(-fp_in[:, f, :].T, far_quant)] * 3
    own_left, own_right = jnp.concatenate(own_left, axis=1), jnp.concatenate(own_right, axis=1)
    far_left, far_right = jnp.concatenate(far_left, axis=1), jnp.concatenate(far_right, axis=1)
    own_mat[...] = triple(kron(own_held, own_left, own_right))
    far_mat[...] = triple(kron(far_held, far_left, far_right))

    def mask_of(lanes):
        piece = jnp.broadcast_to(jnp.where(lanes, 1.0, 0.0), (16, ELEMS)).astype(BF16)
        return jnp.concatenate([piece] * (TRACE // 16), axis=0)

    masks = [[mask_of(turning[f : f + 1] == h) for h in range(3)] for f in range(4)]
    scales = [geo_in[pl.ds(3 + f, 1), :] for f in range(4)]
    blank = jnp.zeros((LANES - ROWS, ELEMS), BF16)

    def correct_near(values):
        hi, lo = split(values)
        traces = nn(
            trace_mat[...], jnp.concatenate([hi, blank, hi, blank, lo, blank], axis=0)
        )
        traces = [traces[TRACE * j : TRACE * (j + 1)] for j in range(4)]
        change = nn(vol_mat[...], scaled_three(values))
        change = change + nn(own_mat[...], stack([split(scales[f] * traces[f]) for f in range(4)]))
        picked = nn(tall(jnp.concatenate(traces, axis=1)), near_hot[...])
        return change, picked[:TRACE] + picked[TRACE:]

    def correct_far(turn, picked):
        hi, lo = split(ghosts[turn])
        traces = nt(trace_mat[...], jnp.concatenate([hi, hi, lo], axis=1))
        chosen = traces[:TRACE]
        for j in range(1, 4):
            chosen = jnp.where(slot_face == j, traces[TRACE * j : TRACE * (j + 1)], chosen)
        received = nn(tall(chosen), ghost_hot[...])
        picked = picked + (received[:TRACE] + received[TRACE:])
        pairs = []
        for f in range(4):
            hi, lo = split(scales[f] * picked[:, ELEMS * f : ELEMS * (f + 1)])
            pairs += [(hi * masks[f][h], lo * masks[f][h]) for h in range(3)]
        return nn(far_mat[...], stack(pairs))

    def finish(copies):
        for copy in copies:
            copy.wait_recv()

    change, picked = correct_near(first_part)
    near_one = x_ref[...] + change
    finish(copies_one)
    halfway = near_one + correct_far(0, picked)
    fine_part = predict(halfway, [(0.0, STEP)])[0]
    loads[13].wait()
    second_part = jnp.where(clu_in[...] == 0, fine_part, late_part)
    copies_two = send(1, second_part)
    change, picked = correct_near(second_part)
    near_two = halfway + change
    finish(copies_two)
    x_ref[...] = near_two + correct_far(1, picked)
    for q in range(QUANT):
        out_ref[q] = x_ref[pl.ds(BASIS * q, BASIS), :]
    for copy in copies_one + copies_two:
        copy.wait_send()


def local(
    solution, geometry, cluster, neighbour, orient, send_elem, stiff_time, stiff_vol, jacobians,
    flux_minus, flux_plus, lifting, restrict, orient_mat,
):
    inner = (1, 0, 2)
    args = (
        solution.transpose(inner), geometry, cluster.reshape(1, ELEMS), neighbour, orient,
        send_elem, stiff_time, stiff_vol, jacobians.transpose(inner),
        flux_minus.transpose(inner), flux_plus.transpose(inner), lifting.transpose(2, 0, 1),
        restrict.transpose(inner), orient_mat.transpose(inner),
    )
    held = [pltpu.VMEM(a.shape, a.dtype) for a in args]
    result = pl.pallas_call(
        kernel,
        out_shape=jax.ShapeDtypeStruct((QUANT, BASIS, ELEMS), F32),
        in_specs=[pl.BlockSpec(memory_space=pl.ANY)] * len(args),
        out_specs=pl.BlockSpec(memory_space=pltpu.VMEM),
        scratch_shapes=held
        + [
            pltpu.VMEM((ROWS, ELEMS), F32),
            pltpu.VMEM((ROWS, 3 * ROWS), F32),
            pltpu.VMEM((ROWS, 3 * ROWS), F32),
            pltpu.VMEM((ROWS, 4 * TRACE), F32),
            pltpu.VMEM((ROWS, 12 * TRACE), F32),
            pltpu.VMEM((4 * TRACE, LANES), F32),
            pltpu.VMEM((ROWS, 9 * ROWS), BF16),
            pltpu.VMEM((ROWS, 9 * ROWS), BF16),
            pltpu.VMEM((ROWS, 12 * TRACE), BF16),
            pltpu.VMEM((ROWS, 36 * TRACE), BF16),
            pltpu.VMEM((4 * TRACE, 3 * LANES), BF16),
            pltpu.VMEM((4 * ELEMS, 4 * ELEMS), BF16),
            pltpu.VMEM((ELEMS, 4 * ELEMS), BF16),
            pltpu.VMEM((2, ELEMS, LANES), F32),
            pltpu.VMEM((2, ELEMS, LANES), F32),
            pltpu.SemaphoreType.DMA((len(args),)),
            pltpu.SemaphoreType.DMA((2, 4)),
            pltpu.SemaphoreType.DMA((2, 4)),
        ],
        compiler_params=pltpu.CompilerParams(
            collective_id=0, has_side_effects=True, vmem_limit_bytes=60 * 1024 * 1024
        ),
    )(*args)
    return result.transpose(inner)


def solution(mesh):
    split_last = P(None, ("dom", "sub"))
    return jax.shard_map(
        local,
        mesh=mesh,
        in_specs=(P(None, None, ("dom", "sub")), split_last, P(("dom", "sub")))
        + (split_last,) * 3
        + (P(),) * 8,
        out_specs=P(None, None, ("dom", "sub")),
        check_vma=False,
    )
```

```python
import functools
import jax
import jax.numpy as jnp
from jax import lax
from jax.experimental import pallas as pl
from jax.experimental.pallas import tpu as pltpu
from jax.sharding import PartitionSpec as P

STEP = 0.4
BASIS = 20
QUANT = 9
ROWS = 192
LANES = 256
TRACE = 96
ELEMS = 128
SLOTS = 32
MESH = pl.DeviceIdType.MESH
F32 = jnp.float32
BF16 = jnp.bfloat16


def nn(a, b):
    return lax.dot_general(a, b, (((1,), (0,)), ((), ())), preferred_element_type=F32)


def nt(a, b):
    return lax.dot_general(a, b, (((1,), (1,)), ((), ())), preferred_element_type=F32)


def split(x):
    hi = x.astype(BF16)
    return hi, (x - hi.astype(F32)).astype(BF16)


def wide(x):
    return jnp.concatenate(split(x), axis=1)


def tall(x):
    return jnp.concatenate(split(x), axis=0)


def onehot(mask):
    return jnp.where(mask, 1.0, 0.0).astype(BF16)


def iota(shape, dim):
    return lax.broadcasted_iota(jnp.int32, shape, dim)


def triple(x):
    hi, lo = split(x)
    return jnp.concatenate([hi, lo, hi], axis=1)


def stack(pairs):
    his = [hi for hi, _ in pairs]
    return jnp.concatenate(his + his + [lo for _, lo in pairs], axis=0)


def spread(x, places):
    hi, lo = split(x)
    return nn(hi, places) + nn(lo, places)


def triple_product(x, y):
    x_hi, x_lo = split(x)
    y_hi, y_lo = split(y)
    return nn(x_hi, y_hi) + (nn(x_hi, y_lo) + nn(x_lo, y_hi))


def kron(held, left, right):
    wide_part = pl.ds(0, left.shape[1])
    for q in range(QUANT):
        held[pl.ds(BASIS * q, BASIS), wide_part] = left * right[q : q + 1]
    held[pl.ds(BASIS * QUANT, ROWS - BASIS * QUANT), wide_part] = jnp.zeros(
        (ROWS - BASIS * QUANT, left.shape[1]), F32
    )
    return held[:, wide_part]


def by_basis(index):
    return (index * 205) >> 12


def by_face_basis(index):
    return (index * 205) >> 11


def kernel(
    x_any, geo_any, clu_any, nb_any, ori_any, snd_any, st_any, sv_any, jac_any, fm_any, fp_any,
    lif_any, res_any, om_any, out_ref,
    x_in, geo_in, clu_in, nb_in, ori_in, snd_in, st_in, sv_in, jac_in, fm_in, fp_in, lif_in,
    res_in, om_in,
    x_ref, time_held, vol_held, own_held, far_held, trace_held, time_mat, vol_mat, own_mat, far_mat,
    trace_mat, near_hot, ghost_hot, outgoing, ghosts,
    in_sem, send_sem, recv_sem,
):
    pairs = [
        (x_any, x_in), (st_any, st_in), (jac_any, jac_in), (geo_any, geo_in), (snd_any, snd_in),
        (res_any, res_in), (nb_any, nb_in), (ori_any, ori_in), (sv_any, sv_in), (fm_any, fm_in),
        (lif_any, lif_in), (om_any, om_in), (fp_any, fp_in), (clu_any, clu_in),
    ]
    loads = []
    for place, (source, target) in enumerate(pairs):
        load = pltpu.make_async_copy(source, target, in_sem.at[place])
        load.start()
        loads.append(load)

    dom, sub = lax.axis_index("dom"), lax.axis_index("sub")
    doms, subs = lax.axis_size("dom"), lax.axis_size("sub")
    dom_up, dom_down = lax.rem(dom + 1, doms), lax.rem(dom + doms - 1, doms)
    sub_up, sub_down = lax.rem(sub + 1, subs), lax.rem(sub + subs - 1, subs)
    targets = [(dom_up, sub), (dom_down, sub), (dom, sub_up), (dom, sub_down)]
    barrier = pltpu.get_barrier_semaphore()
    for target in targets:
        pl.semaphore_signal(barrier, inc=1, device_id=target, device_id_type=MESH)

    col = iota((BASIS, ROWS), 1)
    in_cols = col < BASIS * QUANT
    col_q = by_basis(col)
    col_b = col - BASIS * col_q
    basis_cols = onehot((col_b == iota((BASIS, ROWS), 0)) & in_cols)
    quant_cols = onehot((col_q == iota((BASIS, ROWS), 0)) & in_cols)[:QUANT]

    loads[1].wait()
    loads[2].wait()
    factors = jnp.concatenate([spread(jac_in[:, d, :].T, quant_cols) for d in range(3)], axis=1)
    stiff = jnp.concatenate([spread(st_in[d], basis_cols) for d in range(3)], axis=1)
    time_mat[...] = triple(kron(time_held, stiff, factors))

    loads[0].wait()
    for q in range(QUANT):
        x_ref[pl.ds(BASIS * q, BASIS), :] = x_in[q]
    x_ref[pl.ds(BASIS * QUANT, ROWS - BASIS * QUANT), :] = jnp.zeros(
        (ROWS - BASIS * QUANT, ELEMS), F32
    )
    loads[3].wait()

    def scaled_three(values):
        return stack([split(geo_in[pl.ds(g, 1), :] * values) for g in range(3)])

    def predict(values, spans):
        current = values
        sums = [(b - a) * values for a, b in spans]
        factorial = 1.0
        for degree in range(1, 4):
            current = nn(time_mat[...], scaled_three(current))
            factorial = factorial * (degree + 1)
            sign = -1.0 if degree % 2 else 1.0
            sums = [
                s + (sign * (b ** (degree + 1) - a ** (degree + 1)) / factorial) * current
                for s, (a, b) in zip(sums, spans)
            ]
        return sums

    first_part, late_part = predict(x_ref[...], [(0.0, STEP), (STEP, 2.0 * STEP)])

    loads[4].wait()
    eye = onehot(iota((SLOTS, SLOTS), 0) == iota((SLOTS, SLOTS), 1))
    named = nt(eye, snd_in[...].astype(F32).astype(BF16))
    elem = iota((SLOTS, ELEMS), 1)
    picks = jnp.concatenate(
        [onehot(named[:, d : d + 1].astype(jnp.int32) == elem) for d in range(4)], axis=0
    )
    pick_both = jnp.concatenate([picks, picks], axis=1)

    outgoing[:, :, pl.ds(ROWS, LANES - ROWS)] = jnp.zeros((2, ELEMS, LANES - ROWS), F32)

    def send(turn, values):
        outgoing[turn, :, pl.ds(0, ROWS)] = nt(pick_both, wide(values))
        if turn == 0:
            pl.semaphore_wait(barrier, 4)
        copies = []
        for d in range(4):
            part = pl.ds(SLOTS * d, SLOTS)
            copy = pltpu.make_async_remote_copy(
                src_ref=outgoing.at[turn, part],
                dst_ref=ghosts.at[turn, part],
                send_sem=send_sem.at[turn, d],
                recv_sem=recv_sem.at[turn, d],
                device_id=targets[d],
                device_id_type=MESH,
            )
            copy.start()
            copies.append(copy)
        return copies

    copies_one = send(0, first_part)

    loads[5].wait()
    trace_col = iota((10, LANES), 1)
    trace_q = by_basis(trace_col)
    for j in range(4):
        places = onehot(
            (iota((BASIS, LANES), 1) - BASIS * by_basis(iota((BASIS, LANES), 1)))
            == iota((BASIS, LANES), 0)
        )
        block = spread(res_in[:, j, :], places)
        for q in range(QUANT):
            trace_held[pl.ds(TRACE * j + 10 * q, 10), :] = jnp.where(trace_q == q, block, 0.0)
        trace_held[pl.ds(TRACE * j + 90, TRACE - 90), :] = jnp.zeros((TRACE - 90, LANES), F32)
    trace_mat[...] = triple(trace_held[...])

    loads[6].wait()
    loads[7].wait()
    facing = (ori_in[...] * 11) >> 5
    turning = ori_in[...] - 3 * facing
    behind = nb_in[...]
    near_key = jnp.where(behind < ELEMS, behind + ELEMS * facing, -1)
    key_row = iota((4 * ELEMS, ELEMS), 0)
    slot_row = iota((ELEMS, ELEMS), 0) + ELEMS
    slot_face = jnp.zeros((16, ELEMS), F32)
    for f in range(4):
        part = pl.ds(ELEMS * f, ELEMS)
        near_hot[:, part] = onehot(key_row == near_key[f : f + 1])
        hot = onehot(slot_row == behind[f : f + 1])
        ghost_hot[:, part] = hot
        face = jnp.broadcast_to(facing[f : f + 1].astype(F32), (16, ELEMS)).astype(BF16)
        slot_face = slot_face + nt(face, hot)
    slot_face = slot_face[0:1]

    loads[8].wait()
    stiff = jnp.concatenate([spread(sv_in[d], basis_cols) for d in range(3)], axis=1)
    vol_mat[...] = triple(kron(vol_held, stiff, factors))

    loads[9].wait()
    loads[10].wait()
    loads[11].wait()
    loads[12].wait()
    far_col = iota((16, TRACE), 1)
    far_q = by_face_basis(far_col)
    far_row = iota((16, TRACE), 0)
    far_in = far_col < 90
    far_basis = onehot((far_col - 10 * far_q == far_row) & far_in)[:10]
    far_quant = onehot((far_q == far_row) & far_in)[:QUANT]
    turned = jnp.concatenate([spread(om_in[:, h, :], far_basis) for h in range(3)], axis=1)
    own_left, own_right, far_left, far_right = [], [], [], []
    for f in range(4):
        lifting = lif_in[:, f, :].T
        own_left.append(spread(lifting, far_basis))
        own_right.append(spread(-fm_in[:, f, :].T, far_quant))
        far_left.append(triple_product(lifting, turned))
        far_right += [spread(-fp_in[:, f, :].T, far_quant)] * 3
    own_left, own_right = jnp.concatenate(own_left, axis=1), jnp.concatenate(own_right, axis=1)
    far_left, far_right = jnp.concatenate(far_left, axis=1), jnp.concatenate(far_right, axis=1)
    own_mat[...] = triple(kron(own_held, own_left, own_right))
    far_mat[...] = triple(kron(far_held, far_left, far_right))

    def mask_of(lanes):
        piece = jnp.broadcast_to(jnp.where(lanes, 1.0, 0.0), (16, ELEMS)).astype(BF16)
        return jnp.concatenate([piece] * (TRACE // 16), axis=0)

    masks = [[mask_of(turning[f : f + 1] == h) for h in range(3)] for f in range(4)]
    scales = [geo_in[pl.ds(3 + f, 1), :] for f in range(4)]
    blank = jnp.zeros((LANES - ROWS, ELEMS), BF16)

    def correct_near(values):
        hi, lo = split(values)
        traces = nn(
            trace_mat[...], jnp.concatenate([hi, blank, hi, blank, lo, blank], axis=0)
        )
        traces = [traces[TRACE * j : TRACE * (j + 1)] for j in range(4)]
        change = nn(vol_mat[...], scaled_three(values))
        change = change + nn(own_mat[...], stack([split(scales[f] * traces[f]) for f in range(4)]))
        picked = nn(tall(jnp.concatenate(traces, axis=1)), near_hot[...])
        return change, picked[:TRACE] + picked[TRACE:]

    def correct_far(turn, picked):
        hi, lo = split(ghosts[turn])
        traces = nt(trace_mat[...], jnp.concatenate([hi, hi, lo], axis=1))
        chosen = traces[:TRACE]
        for j in range(1, 4):
            chosen = jnp.where(slot_face == j, traces[TRACE * j : TRACE * (j + 1)], chosen)
        received = nn(tall(chosen), ghost_hot[...])
        picked = picked + (received[:TRACE] + received[TRACE:])
        pairs = []
        for f in range(4):
            hi, lo = split(scales[f] * picked[:, ELEMS * f : ELEMS * (f + 1)])
            pairs += [(hi * masks[f][h], lo * masks[f][h]) for h in range(3)]
        return nn(far_mat[...], stack(pairs))

    def finish(copies):
        for copy in copies:
            copy.wait_recv()

    change, picked = correct_near(first_part)
    near_one = x_ref[...] + change
    finish(copies_one)
    halfway = near_one + correct_far(0, picked)
    fine_part = predict(halfway, [(0.0, STEP)])[0]
    loads[13].wait()
    second_part = jnp.where(clu_in[...] == 0, fine_part, late_part)
    copies_two = send(1, second_part)
    change, picked = correct_near(second_part)
    near_two = halfway + change
    finish(copies_two)
    x_ref[...] = near_two + correct_far(1, picked)
    for q in range(QUANT):
        out_ref[q] = x_ref[pl.ds(BASIS * q, BASIS), :]
    for copy in copies_one + copies_two:
        copy.wait_send()


def local(
    solution, geometry, cluster, neighbour, orient, send_elem, stiff_time, stiff_vol, jacobians,
    flux_minus, flux_plus, lifting, restrict, orient_mat,
):
    inner = (1, 0, 2)
    args = (
        solution.transpose(inner), geometry, cluster.reshape(1, ELEMS), neighbour, orient,
        send_elem, stiff_time, stiff_vol, jacobians.transpose(inner),
        flux_minus.transpose(inner), flux_plus.transpose(inner), lifting.transpose(2, 0, 1),
        restrict.transpose(inner), orient_mat.transpose(inner),
    )
    held = [pltpu.VMEM(a.shape, a.dtype) for a in args]
    result = pl.pallas_call(
        kernel,
        out_shape=pltpu.VMEM((QUANT, BASIS, ELEMS), F32),
        in_specs=[pl.BlockSpec(memory_space=pl.ANY)] * len(args),
        out_specs=pl.BlockSpec(memory_space=pltpu.VMEM),
        scratch_shapes=held
        + [
            pltpu.VMEM((ROWS, ELEMS), F32),
            pltpu.VMEM((ROWS, 3 * ROWS), F32),
            pltpu.VMEM((ROWS, 3 * ROWS), F32),
            pltpu.VMEM((ROWS, 4 * TRACE), F32),
            pltpu.VMEM((ROWS, 12 * TRACE), F32),
            pltpu.VMEM((4 * TRACE, LANES), F32),
            pltpu.VMEM((ROWS, 9 * ROWS), BF16),
            pltpu.VMEM((ROWS, 9 * ROWS), BF16),
            pltpu.VMEM((ROWS, 12 * TRACE), BF16),
            pltpu.VMEM((ROWS, 36 * TRACE), BF16),
            pltpu.VMEM((4 * TRACE, 3 * LANES), BF16),
            pltpu.VMEM((4 * ELEMS, 4 * ELEMS), BF16),
            pltpu.VMEM((ELEMS, 4 * ELEMS), BF16),
            pltpu.VMEM((2, ELEMS, LANES), F32),
            pltpu.VMEM((2, ELEMS, LANES), F32),
            pltpu.SemaphoreType.DMA((len(args),)),
            pltpu.SemaphoreType.DMA((2, 4)),
            pltpu.SemaphoreType.DMA((2, 4)),
        ],
        compiler_params=pltpu.CompilerParams(
            collective_id=0, has_side_effects=True, vmem_limit_bytes=55 * 1024 * 1024
        ),
    )(*args)
    return result.transpose(inner)


def solution(mesh):
    split_last = P(None, ("dom", "sub"))
    return jax.shard_map(
        local,
        mesh=mesh,
        in_specs=(P(None, None, ("dom", "sub")), split_last, P(("dom", "sub")))
        + (split_last,) * 3
        + (P(),) * 8,
        out_specs=P(None, None, ("dom", "sub")),
        check_vma=False,
    )
```

```python
import functools
import jax
import jax.numpy as jnp
from jax import lax
from jax.experimental import pallas as pl
from jax.experimental.pallas import tpu as pltpu
from jax.sharding import PartitionSpec as P

STEP = 0.4
BASIS = 20
QUANT = 9
ROWS = 192
LANES = 256
TRACE = 96
ELEMS = 128
SLOTS = 32
MESH = pl.DeviceIdType.MESH
F32 = jnp.float32
BF16 = jnp.bfloat16


def nn(a, b):
    return lax.dot_general(a, b, (((1,), (0,)), ((), ())), preferred_element_type=F32)


def nt(a, b):
    return lax.dot_general(a, b, (((1,), (1,)), ((), ())), preferred_element_type=F32)


def split(x):
    hi = x.astype(BF16)
    return hi, (x - hi.astype(F32)).astype(BF16)


def wide(x):
    return jnp.concatenate(split(x), axis=1)


def tall(x):
    return jnp.concatenate(split(x), axis=0)


def onehot(mask):
    return jnp.where(mask, 1.0, 0.0).astype(BF16)


def iota(shape, dim):
    return lax.broadcasted_iota(jnp.int32, shape, dim)


def triple(x):
    hi, lo = split(x)
    return jnp.concatenate([hi, lo, hi], axis=1)


def stack(pairs):
    his = [hi for hi, _ in pairs]
    return jnp.concatenate(his + his + [lo for _, lo in pairs], axis=0)


def spread(x, places):
    hi, lo = split(x)
    return nn(hi, places) + nn(lo, places)


def triple_product(x, y):
    x_hi, x_lo = split(x)
    y_hi, y_lo = split(y)
    return nn(x_hi, y_hi) + (nn(x_hi, y_lo) + nn(x_lo, y_hi))


def kron(held, left, right):
    wide_part = pl.ds(0, left.shape[1])
    for q in range(QUANT):
        held[pl.ds(BASIS * q, BASIS), wide_part] = left * right[q : q + 1]
    held[pl.ds(BASIS * QUANT, ROWS - BASIS * QUANT), wide_part] = jnp.zeros(
        (ROWS - BASIS * QUANT, left.shape[1]), F32
    )
    return held[:, wide_part]


def by_basis(index):
    return (index * 205) >> 12


def by_face_basis(index):
    return (index * 205) >> 11


def kernel(
    x_any, geo_any, clu_any, nb_any, ori_any, snd_any, st_any, sv_any, jac_any, fm_any, fp_any,
    lif_any, res_any, om_any, out_ref,
    x_in, geo_in, clu_in, nb_in, ori_in, snd_in, st_in, sv_in, jac_in, fm_in, fp_in, lif_in,
    res_in, om_in,
    x_ref, time_held, vol_held, own_held, far_held, trace_held, time_mat, vol_mat, own_mat, far_mat,
    trace_mat, near_hot, ghost_hot, outgoing, ghosts,
    in_sem, send_sem, recv_sem,
):
    pairs = [
        (x_any, x_in), (st_any, st_in), (jac_any, jac_in), (geo_any, geo_in), (snd_any, snd_in),
        (res_any, res_in), (nb_any, nb_in), (ori_any, ori_in), (sv_any, sv_in), (fm_any, fm_in),
        (lif_any, lif_in), (om_any, om_in), (fp_any, fp_in), (clu_any, clu_in),
    ]
    loads = []
    for place, (source, target) in enumerate(pairs):
        load = pltpu.make_async_copy(source, target, in_sem.at[place])
        load.start()
        loads.append(load)

    dom, sub = lax.axis_index("dom"), lax.axis_index("sub")
    doms, subs = lax.axis_size("dom"), lax.axis_size("sub")
    dom_up, dom_down = lax.rem(dom + 1, doms), lax.rem(dom + doms - 1, doms)
    sub_up, sub_down = lax.rem(sub + 1, subs), lax.rem(sub + subs - 1, subs)
    targets = [(dom_up, sub), (dom_down, sub), (dom, sub_up), (dom, sub_down)]
    below, above = dom > 0, dom < doms - 1
    sends, arrives = [above, below, None, None], [below, above, None, None]
    ghosts[:, pl.ds(0, 2 * SLOTS), :] = jnp.zeros((2, 2 * SLOTS, LANES), F32)

    def where_any(condition, action):
        if condition is None:
            action()
        else:
            pl.when(condition)(action)

    barrier = pltpu.get_barrier_semaphore()
    for d in range(4):
        where_any(
            sends[d],
            functools.partial(
                pl.semaphore_signal, barrier, inc=1, device_id=targets[d], device_id_type=MESH
            ),
        )

    col = iota((BASIS, ROWS), 1)
    in_cols = col < BASIS * QUANT
    col_q = by_basis(col)
    col_b = col - BASIS * col_q
    basis_cols = onehot((col_b == iota((BASIS, ROWS), 0)) & in_cols)
    quant_cols = onehot((col_q == iota((BASIS, ROWS), 0)) & in_cols)[:QUANT]

    loads[1].wait()
    loads[2].wait()
    factors = jnp.concatenate([spread(jac_in[:, d, :].T, quant_cols) for d in range(3)], axis=1)
    stiff = jnp.concatenate([spread(st_in[d], basis_cols) for d in range(3)], axis=1)
    time_mat[...] = triple(kron(time_held, stiff, factors))

    loads[0].wait()
    for q in range(QUANT):
        x_ref[pl.ds(BASIS * q, BASIS), :] = x_in[q]
    x_ref[pl.ds(BASIS * QUANT, ROWS - BASIS * QUANT), :] = jnp.zeros(
        (ROWS - BASIS * QUANT, ELEMS), F32
    )
    loads[3].wait()

    def scaled_three(values):
        return stack([split(geo_in[pl.ds(g, 1), :] * values) for g in range(3)])

    def predict(values, spans):
        current = values
        sums = [(b - a) * values for a, b in spans]
        factorial = 1.0
        for degree in range(1, 4):
            current = nn(time_mat[...], scaled_three(current))
            factorial = factorial * (degree + 1)
            sign = -1.0 if degree % 2 else 1.0
            sums = [
                s + (sign * (b ** (degree + 1) - a ** (degree + 1)) / factorial) * current
                for s, (a, b) in zip(sums, spans)
            ]
        return sums

    first_part, late_part = predict(x_ref[...], [(0.0, STEP), (STEP, 2.0 * STEP)])

    loads[4].wait()
    eye = onehot(iota((SLOTS, SLOTS), 0) == iota((SLOTS, SLOTS), 1))
    named = nt(eye, snd_in[...].astype(F32).astype(BF16))
    elem = iota((SLOTS, ELEMS), 1)
    picks = jnp.concatenate(
        [onehot(named[:, d : d + 1].astype(jnp.int32) == elem) for d in range(4)], axis=0
    )
    pick_both = jnp.concatenate([picks, picks], axis=1)

    outgoing[:, :, pl.ds(ROWS, LANES - ROWS)] = jnp.zeros((2, ELEMS, LANES - ROWS), F32)

    def send(turn, values):
        outgoing[turn, :, pl.ds(0, ROWS)] = nt(pick_both, wide(values))
        if turn == 0:
            pl.semaphore_wait(barrier, 2 + below.astype(jnp.int32) + above.astype(jnp.int32))
        copies = []
        for d in range(4):
            part = pl.ds(SLOTS * d, SLOTS)
            copy = pltpu.make_async_remote_copy(
                src_ref=outgoing.at[turn, part],
                dst_ref=ghosts.at[turn, part],
                send_sem=send_sem.at[turn, d],
                recv_sem=recv_sem.at[turn, d],
                device_id=targets[d],
                device_id_type=MESH,
            )
            where_any(sends[d], copy.start)
            copies.append(copy)
        return copies

    copies_one = send(0, first_part)

    loads[5].wait()
    trace_col = iota((10, LANES), 1)
    trace_q = by_basis(trace_col)
    for j in range(4):
        places = onehot(
            (iota((BASIS, LANES), 1) - BASIS * by_basis(iota((BASIS, LANES), 1)))
            == iota((BASIS, LANES), 0)
        )
        block = spread(res_in[:, j, :], places)
        for q in range(QUANT):
            trace_held[pl.ds(TRACE * j + 10 * q, 10), :] = jnp.where(trace_q == q, block, 0.0)
        trace_held[pl.ds(TRACE * j + 90, TRACE - 90), :] = jnp.zeros((TRACE - 90, LANES), F32)
    trace_mat[...] = triple(trace_held[...])

    loads[6].wait()
    loads[7].wait()
    facing = (ori_in[...] * 11) >> 5
    turning = ori_in[...] - 3 * facing
    behind = nb_in[...]
    near_key = jnp.where(behind < ELEMS, behind + ELEMS * facing, -1)
    key_row = iota((4 * ELEMS, ELEMS), 0)
    slot_row = iota((ELEMS, ELEMS), 0) + ELEMS
    slot_face = jnp.zeros((16, ELEMS), F32)
    for f in range(4):
        part = pl.ds(ELEMS * f, ELEMS)
        near_hot[:, part] = onehot(key_row == near_key[f : f + 1])
        hot = onehot(slot_row == behind[f : f + 1])
        ghost_hot[:, part] = hot
        face = jnp.broadcast_to(facing[f : f + 1].astype(F32), (16, ELEMS)).astype(BF16)
        slot_face = slot_face + nt(face, hot)
    slot_face = slot_face[0:1]

    loads[8].wait()
    stiff = jnp.concatenate([spread(sv_in[d], basis_cols) for d in range(3)], axis=1)
    vol_mat[...] = triple(kron(vol_held, stiff, factors))

    loads[9].wait()
    loads[10].wait()
    loads[11].wait()
    loads[12].wait()
    far_col = iota((16, TRACE), 1)
    far_q = by_face_basis(far_col)
    far_row = iota((16, TRACE), 0)
    far_in = far_col < 90
    far_basis = onehot((far_col - 10 * far_q == far_row) & far_in)[:10]
    far_quant = onehot((far_q == far_row) & far_in)[:QUANT]
    turned = jnp.concatenate([spread(om_in[:, h, :], far_basis) for h in range(3)], axis=1)
    own_left, own_right, far_left, far_right = [], [], [], []
    for f in range(4):
        lifting = lif_in[:, f, :].T
        own_left.append(spread(lifting, far_basis))
        own_right.append(spread(-fm_in[:, f, :].T, far_quant))
        far_left.append(triple_product(lifting, turned))
        far_right += [spread(-fp_in[:, f, :].T, far_quant)] * 3
    own_left, own_right = jnp.concatenate(own_left, axis=1), jnp.concatenate(own_right, axis=1)
    far_left, far_right = jnp.concatenate(far_left, axis=1), jnp.concatenate(far_right, axis=1)
    own_mat[...] = triple(kron(own_held, own_left, own_right))
    far_mat[...] = triple(kron(far_held, far_left, far_right))

    def mask_of(lanes):
        piece = jnp.broadcast_to(jnp.where(lanes, 1.0, 0.0), (16, ELEMS)).astype(BF16)
        return jnp.concatenate([piece] * (TRACE // 16), axis=0)

    masks = [[mask_of(turning[f : f + 1] == h) for h in range(3)] for f in range(4)]
    scales = [geo_in[pl.ds(3 + f, 1), :] for f in range(4)]
    blank = jnp.zeros((LANES - ROWS, ELEMS), BF16)

    def correct_near(values):
        hi, lo = split(values)
        traces = nn(
            trace_mat[...], jnp.concatenate([hi, blank, hi, blank, lo, blank], axis=0)
        )
        traces = [traces[TRACE * j : TRACE * (j + 1)] for j in range(4)]
        change = nn(vol_mat[...], scaled_three(values))
        change = change + nn(own_mat[...], stack([split(scales[f] * traces[f]) for f in range(4)]))
        picked = nn(tall(jnp.concatenate(traces, axis=1)), near_hot[...])
        return change, picked[:TRACE] + picked[TRACE:]

    def correct_far(turn, picked):
        hi, lo = split(ghosts[turn])
        traces = nt(trace_mat[...], jnp.concatenate([hi, hi, lo], axis=1))
        chosen = traces[:TRACE]
        for j in range(1, 4):
            chosen = jnp.where(slot_face == j, traces[TRACE * j : TRACE * (j + 1)], chosen)
        received = nn(tall(chosen), ghost_hot[...])
        picked = picked + (received[:TRACE] + received[TRACE:])
        pairs = []
        for f in range(4):
            hi, lo = split(scales[f] * picked[:, ELEMS * f : ELEMS * (f + 1)])
            pairs += [(hi * masks[f][h], lo * masks[f][h]) for h in range(3)]
        return nn(far_mat[...], stack(pairs))

    def finish(copies):
        for d in range(4):
            where_any(arrives[d], copies[d].wait_recv)

    change, picked = correct_near(first_part)
    near_one = x_ref[...] + change
    finish(copies_one)
    halfway = near_one + correct_far(0, picked)
    fine_part = predict(halfway, [(0.0, STEP)])[0]
    loads[13].wait()
    second_part = jnp.where(clu_in[...] == 0, fine_part, late_part)
    copies_two = send(1, second_part)
    change, picked = correct_near(second_part)
    near_two = halfway + change
    finish(copies_two)
    x_ref[...] = near_two + correct_far(1, picked)
    for q in range(QUANT):
        out_ref[q] = x_ref[pl.ds(BASIS * q, BASIS), :]
    for copies in (copies_one, copies_two):
        for d in range(4):
            where_any(sends[d], copies[d].wait_send)


def local(
    solution, geometry, cluster, neighbour, orient, send_elem, stiff_time, stiff_vol, jacobians,
    flux_minus, flux_plus, lifting, restrict, orient_mat,
):
    inner = (1, 0, 2)
    args = (
        solution.transpose(inner), geometry, cluster.reshape(1, ELEMS), neighbour, orient,
        send_elem, stiff_time, stiff_vol, jacobians.transpose(inner),
        flux_minus.transpose(inner), flux_plus.transpose(inner), lifting.transpose(2, 0, 1),
        restrict.transpose(inner), orient_mat.transpose(inner),
    )
    held = [pltpu.VMEM(a.shape, a.dtype) for a in args]
    result = pl.pallas_call(
        kernel,
        out_shape=pltpu.VMEM((QUANT, BASIS, ELEMS), F32),
        in_specs=[pl.BlockSpec(memory_space=pl.ANY)] * len(args),
        out_specs=pl.BlockSpec(memory_space=pltpu.VMEM),
        scratch_shapes=held
        + [
            pltpu.VMEM((ROWS, ELEMS), F32),
            pltpu.VMEM((ROWS, 3 * ROWS), F32),
            pltpu.VMEM((ROWS, 3 * ROWS), F32),
            pltpu.VMEM((ROWS, 4 * TRACE), F32),
            pltpu.VMEM((ROWS, 12 * TRACE), F32),
            pltpu.VMEM((4 * TRACE, LANES), F32),
            pltpu.VMEM((ROWS, 9 * ROWS), BF16),
            pltpu.VMEM((ROWS, 9 * ROWS), BF16),
            pltpu.VMEM((ROWS, 12 * TRACE), BF16),
            pltpu.VMEM((ROWS, 36 * TRACE), BF16),
            pltpu.VMEM((4 * TRACE, 3 * LANES), BF16),
            pltpu.VMEM((4 * ELEMS, 4 * ELEMS), BF16),
            pltpu.VMEM((ELEMS, 4 * ELEMS), BF16),
            pltpu.VMEM((2, ELEMS, LANES), F32),
            pltpu.VMEM((2, ELEMS, LANES), F32),
            pltpu.SemaphoreType.DMA((len(args),)),
            pltpu.SemaphoreType.DMA((2, 4)),
            pltpu.SemaphoreType.DMA((2, 4)),
        ],
        compiler_params=pltpu.CompilerParams(
            collective_id=0, has_side_effects=True, vmem_limit_bytes=55 * 1024 * 1024
        ),
    )(*args)
    return result.transpose(inner)


def solution(mesh):
    split_last = P(None, ("dom", "sub"))
    return jax.shard_map(
        local,
        mesh=mesh,
        in_specs=(P(None, None, ("dom", "sub")), split_last, P(("dom", "sub")))
        + (split_last,) * 3
        + (P(),) * 8,
        out_specs=P(None, None, ("dom", "sub")),
        check_vma=False,
    )
```

```python
import functools
import jax
import jax.numpy as jnp
from jax import lax
from jax.experimental import pallas as pl
from jax.experimental.pallas import tpu as pltpu
from jax.sharding import PartitionSpec as P

STEP = 0.4
BASIS = 20
QUANT = 9
ROWS = 192
LANES = 256
TRACE = 96
ELEMS = 128
SLOTS = 32
MESH = pl.DeviceIdType.MESH
F32 = jnp.float32
BF16 = jnp.bfloat16


def nn(a, b):
    return lax.dot_general(a, b, (((1,), (0,)), ((), ())), preferred_element_type=F32)


def nt(a, b):
    return lax.dot_general(a, b, (((1,), (1,)), ((), ())), preferred_element_type=F32)


def split(x):
    hi = x.astype(BF16)
    return hi, (x - hi.astype(F32)).astype(BF16)


def wide(x):
    return jnp.concatenate(split(x), axis=1)


def tall(x):
    return jnp.concatenate(split(x), axis=0)


def onehot(mask):
    return jnp.where(mask, 1.0, 0.0).astype(BF16)


def iota(shape, dim):
    return lax.broadcasted_iota(jnp.int32, shape, dim)


def triple(x):
    hi, lo = split(x)
    return jnp.concatenate([hi, lo, hi], axis=1)


def stack(pairs):
    his = [hi for hi, _ in pairs]
    return jnp.concatenate(his + his + [lo for _, lo in pairs], axis=0)


def spread(x, places):
    hi, lo = split(x)
    return nn(hi, places) + nn(lo, places)


def triple_product(x, y):
    x_hi, x_lo = split(x)
    y_hi, y_lo = split(y)
    return nn(x_hi, y_hi) + (nn(x_hi, y_lo) + nn(x_lo, y_hi))


def kron(held, left, right):
    wide_part = pl.ds(0, left.shape[1])
    for q in range(QUANT):
        held[pl.ds(BASIS * q, BASIS), wide_part] = left * right[q : q + 1]
    held[pl.ds(BASIS * QUANT, ROWS - BASIS * QUANT), wide_part] = jnp.zeros(
        (ROWS - BASIS * QUANT, left.shape[1]), F32
    )
    return held[:, wide_part]


def by_basis(index):
    return (index * 205) >> 12


def by_face_basis(index):
    return (index * 205) >> 11


def kernel(
    x_any, geo_any, clu_any, nb_any, ori_any, snd_any, st_any, sv_any, jac_any, fm_any, fp_any,
    lif_any, res_any, om_any, out_ref,
    x_in, geo_in, clu_in, nb_in, ori_in, snd_in, st_in, sv_in, jac_in, fm_in, fp_in, lif_in,
    res_in, om_in,
    x_ref, time_held, vol_held, own_held, far_held, trace_held, time_mat, vol_mat, own_mat, far_mat,
    trace_mat, near_hot, ghost_hot, outgoing, ghosts,
    in_sem, send_sem, recv_sem,
):
    pairs = [
        (x_any, x_in), (st_any, st_in), (jac_any, jac_in), (geo_any, geo_in), (snd_any, snd_in),
        (res_any, res_in), (nb_any, nb_in), (ori_any, ori_in), (sv_any, sv_in), (fm_any, fm_in),
        (lif_any, lif_in), (om_any, om_in), (fp_any, fp_in), (clu_any, clu_in),
    ]
    loads = []
    for place, (source, target) in enumerate(pairs):
        load = pltpu.make_async_copy(source, target, in_sem.at[place])
        load.start()
        loads.append(load)

    dom, sub = lax.axis_index("dom"), lax.axis_index("sub")
    doms, subs = lax.axis_size("dom"), lax.axis_size("sub")
    dom_up, dom_down = lax.rem(dom + 1, doms), lax.rem(dom + doms - 1, doms)
    sub_up, sub_down = lax.rem(sub + 1, subs), lax.rem(sub + subs - 1, subs)
    targets = [(dom_up, sub), (dom_down, sub), (dom, sub_up), (dom, sub_down)]
    below, above, left, right = dom > 0, dom < doms - 1, sub > 0, sub < subs - 1
    sends, arrives = [above, below, right, left], [below, above, left, right]
    partners = sum(exists.astype(jnp.int32) for exists in sends)
    ghosts[...] = jnp.zeros((2, ELEMS, LANES), F32)

    barrier = pltpu.get_barrier_semaphore()
    for d in range(4):
        pl.when(sends[d])(
            functools.partial(
                pl.semaphore_signal, barrier, inc=1, device_id=targets[d], device_id_type=MESH
            )
        )

    col = iota((BASIS, ROWS), 1)
    in_cols = col < BASIS * QUANT
    col_q = by_basis(col)
    col_b = col - BASIS * col_q
    basis_cols = onehot((col_b == iota((BASIS, ROWS), 0)) & in_cols)
    quant_cols = onehot((col_q == iota((BASIS, ROWS), 0)) & in_cols)[:QUANT]

    loads[1].wait()
    loads[2].wait()
    factors = jnp.concatenate([spread(jac_in[:, d, :].T, quant_cols) for d in range(3)], axis=1)
    stiff = jnp.concatenate([spread(st_in[d], basis_cols) for d in range(3)], axis=1)
    time_mat[...] = triple(kron(time_held, stiff, factors))

    loads[0].wait()
    for q in range(QUANT):
        x_ref[pl.ds(BASIS * q, BASIS), :] = x_in[q]
    x_ref[pl.ds(BASIS * QUANT, ROWS - BASIS * QUANT), :] = jnp.zeros(
        (ROWS - BASIS * QUANT, ELEMS), F32
    )
    loads[3].wait()

    def scaled_three(values):
        return stack([split(geo_in[pl.ds(g, 1), :] * values) for g in range(3)])

    def predict(values, spans):
        current = values
        sums = [(b - a) * values for a, b in spans]
        factorial = 1.0
        for degree in range(1, 4):
            current = nn(time_mat[...], scaled_three(current))
            factorial = factorial * (degree + 1)
            sign = -1.0 if degree % 2 else 1.0
            sums = [
                s + (sign * (b ** (degree + 1) - a ** (degree + 1)) / factorial) * current
                for s, (a, b) in zip(sums, spans)
            ]
        return sums

    first_part, late_part = predict(x_ref[...], [(0.0, STEP), (STEP, 2.0 * STEP)])

    loads[4].wait()
    eye = onehot(iota((SLOTS, SLOTS), 0) == iota((SLOTS, SLOTS), 1))
    named = nt(eye, snd_in[...].astype(F32).astype(BF16))
    elem = iota((SLOTS, ELEMS), 1)
    picks = jnp.concatenate(
        [onehot(named[:, d : d + 1].astype(jnp.int32) == elem) for d in range(4)], axis=0
    )
    pick_both = jnp.concatenate([picks, picks], axis=1)

    outgoing[:, :, pl.ds(ROWS, LANES - ROWS)] = jnp.zeros((2, ELEMS, LANES - ROWS), F32)

    def send(turn, values):
        outgoing[turn, :, pl.ds(0, ROWS)] = nt(pick_both, wide(values))
        if turn == 0:
            pl.semaphore_wait(barrier, partners)
        copies = []
        for d in range(4):
            part = pl.ds(SLOTS * d, SLOTS)
            copy = pltpu.make_async_remote_copy(
                src_ref=outgoing.at[turn, part],
                dst_ref=ghosts.at[turn, part],
                send_sem=send_sem.at[turn, d],
                recv_sem=recv_sem.at[turn, d],
                device_id=targets[d],
                device_id_type=MESH,
            )
            pl.when(sends[d])(copy.start)
            copies.append(copy)
        return copies

    copies_one = send(0, first_part)

    loads[5].wait()
    trace_col = iota((10, LANES), 1)
    trace_q = by_basis(trace_col)
    for j in range(4):
        places = onehot(
            (iota((BASIS, LANES), 1) - BASIS * by_basis(iota((BASIS, LANES), 1)))
            == iota((BASIS, LANES), 0)
        )
        block = spread(res_in[:, j, :], places)
        for q in range(QUANT):
            trace_held[pl.ds(TRACE * j + 10 * q, 10), :] = jnp.where(trace_q == q, block, 0.0)
        trace_held[pl.ds(TRACE * j + 90, TRACE - 90), :] = jnp.zeros((TRACE - 90, LANES), F32)
    trace_mat[...] = triple(trace_held[...])

    loads[6].wait()
    loads[7].wait()
    facing = (ori_in[...] * 11) >> 5
    turning = ori_in[...] - 3 * facing
    behind = nb_in[...]
    near_key = jnp.where(behind < ELEMS, behind + ELEMS * facing, -1)
    key_row = iota((4 * ELEMS, ELEMS), 0)
    slot_row = iota((ELEMS, ELEMS), 0) + ELEMS
    slot_face = jnp.zeros((16, ELEMS), F32)
    for f in range(4):
        part = pl.ds(ELEMS * f, ELEMS)
        near_hot[:, part] = onehot(key_row == near_key[f : f + 1])
        hot = onehot(slot_row == behind[f : f + 1])
        ghost_hot[:, part] = hot
        face = jnp.broadcast_to(facing[f : f + 1].astype(F32), (16, ELEMS)).astype(BF16)
        slot_face = slot_face + nt(face, hot)
    slot_face = slot_face[0:1]

    loads[8].wait()
    stiff = jnp.concatenate([spread(sv_in[d], basis_cols) for d in range(3)], axis=1)
    vol_mat[...] = triple(kron(vol_held, stiff, factors))

    loads[9].wait()
    loads[10].wait()
    loads[11].wait()
    loads[12].wait()
    far_col = iota((16, TRACE), 1)
    far_q = by_face_basis(far_col)
    far_row = iota((16, TRACE), 0)
    far_in = far_col < 90
    far_basis = onehot((far_col - 10 * far_q == far_row) & far_in)[:10]
    far_quant = onehot((far_q == far_row) & far_in)[:QUANT]
    turned = jnp.concatenate([spread(om_in[:, h, :], far_basis) for h in range(3)], axis=1)
    own_left, own_right, far_left, far_right = [], [], [], []
    for f in range(4):
        lifting = lif_in[:, f, :].T
        own_left.append(spread(lifting, far_basis))
        own_right.append(spread(-fm_in[:, f, :].T, far_quant))
        far_left.append(triple_product(lifting, turned))
        far_right += [spread(-fp_in[:, f, :].T, far_quant)] * 3
    own_left, own_right = jnp.concatenate(own_left, axis=1), jnp.concatenate(own_right, axis=1)
    far_left, far_right = jnp.concatenate(far_left, axis=1), jnp.concatenate(far_right, axis=1)
    own_mat[...] = triple(kron(own_held, own_left, own_right))
    far_mat[...] = triple(kron(far_held, far_left, far_right))

    def mask_of(lanes):
        piece = jnp.broadcast_to(jnp.where(lanes, 1.0, 0.0), (16, ELEMS)).astype(BF16)
        return jnp.concatenate([piece] * (TRACE // 16), axis=0)

    masks = [[mask_of(turning[f : f + 1] == h) for h in range(3)] for f in range(4)]
    scales = [geo_in[pl.ds(3 + f, 1), :] for f in range(4)]
    blank = jnp.zeros((LANES - ROWS, ELEMS), BF16)

    def correct_near(values):
        hi, lo = split(values)
        traces = nn(
            trace_mat[...], jnp.concatenate([hi, blank, hi, blank, lo, blank], axis=0)
        )
        traces = [traces[TRACE * j : TRACE * (j + 1)] for j in range(4)]
        change = nn(vol_mat[...], scaled_three(values))
        change = change + nn(own_mat[...], stack([split(scales[f] * traces[f]) for f in range(4)]))
        picked = nn(tall(jnp.concatenate(traces, axis=1)), near_hot[...])
        return change, picked[:TRACE] + picked[TRACE:]

    def correct_far(turn, picked):
        hi, lo = split(ghosts[turn])
        traces = nt(trace_mat[...], jnp.concatenate([hi, hi, lo], axis=1))
        chosen = traces[:TRACE]
        for j in range(1, 4):
            chosen = jnp.where(slot_face == j, traces[TRACE * j : TRACE * (j + 1)], chosen)
        received = nn(tall(chosen), ghost_hot[...])
        picked = picked + (received[:TRACE] + received[TRACE:])
        pairs = []
        for f in range(4):
            hi, lo = split(scales[f] * picked[:, ELEMS * f : ELEMS * (f + 1)])
            pairs += [(hi * masks[f][h], lo * masks[f][h]) for h in range(3)]
        return nn(far_mat[...], stack(pairs))

    def finish(copies):
        for d in range(4):
            pl.when(arrives[d])(copies[d].wait_recv)

    change, picked = correct_near(first_part)
    near_one = x_ref[...] + change
    finish(copies_one)
    halfway = near_one + correct_far(0, picked)
    fine_part = predict(halfway, [(0.0, STEP)])[0]
    loads[13].wait()
    second_part = jnp.where(clu_in[...] == 0, fine_part, late_part)
    copies_two = send(1, second_part)
    change, picked = correct_near(second_part)
    near_two = halfway + change
    finish(copies_two)
    x_ref[...] = near_two + correct_far(1, picked)
    for q in range(QUANT):
        out_ref[q] = x_ref[pl.ds(BASIS * q, BASIS), :]
    for copies in (copies_one, copies_two):
        for d in range(4):
            pl.when(sends[d])(copies[d].wait_send)


def local(
    solution, geometry, cluster, neighbour, orient, send_elem, stiff_time, stiff_vol, jacobians,
    flux_minus, flux_plus, lifting, restrict, orient_mat,
):
    inner = (1, 0, 2)
    args = (
        solution.transpose(inner), geometry, cluster.reshape(1, ELEMS), neighbour, orient,
        send_elem, stiff_time, stiff_vol, jacobians.transpose(inner),
        flux_minus.transpose(inner), flux_plus.transpose(inner), lifting.transpose(2, 0, 1),
        restrict.transpose(inner), orient_mat.transpose(inner),
    )
    held = [pltpu.VMEM(a.shape, a.dtype) for a in args]
    result = pl.pallas_call(
        kernel,
        out_shape=pltpu.VMEM((QUANT, BASIS, ELEMS), F32),
        in_specs=[pl.BlockSpec(memory_space=pl.ANY)] * len(args),
        out_specs=pl.BlockSpec(memory_space=pltpu.VMEM),
        scratch_shapes=held
        + [
            pltpu.VMEM((ROWS, ELEMS), F32),
            pltpu.VMEM((ROWS, 3 * ROWS), F32),
            pltpu.VMEM((ROWS, 3 * ROWS), F32),
            pltpu.VMEM((ROWS, 4 * TRACE), F32),
            pltpu.VMEM((ROWS, 12 * TRACE), F32),
            pltpu.VMEM((4 * TRACE, LANES), F32),
            pltpu.VMEM((ROWS, 9 * ROWS), BF16),
            pltpu.VMEM((ROWS, 9 * ROWS), BF16),
            pltpu.VMEM((ROWS, 12 * TRACE), BF16),
            pltpu.VMEM((ROWS, 36 * TRACE), BF16),
            pltpu.VMEM((4 * TRACE, 3 * LANES), BF16),
            pltpu.VMEM((4 * ELEMS, 4 * ELEMS), BF16),
            pltpu.VMEM((ELEMS, 4 * ELEMS), BF16),
            pltpu.VMEM((2, ELEMS, LANES), F32),
            pltpu.VMEM((2, ELEMS, LANES), F32),
            pltpu.SemaphoreType.DMA((len(args),)),
            pltpu.SemaphoreType.DMA((2, 4)),
            pltpu.SemaphoreType.DMA((2, 4)),
        ],
        compiler_params=pltpu.CompilerParams(
            collective_id=0, has_side_effects=True, vmem_limit_bytes=55 * 1024 * 1024
        ),
    )(*args)
    return result.transpose(inner)


def solution(mesh):
    split_last = P(None, ("dom", "sub"))
    return jax.shard_map(
        local,
        mesh=mesh,
        in_specs=(P(None, None, ("dom", "sub")), split_last, P(("dom", "sub")))
        + (split_last,) * 3
        + (P(),) * 8,
        out_specs=P(None, None, ("dom", "sub")),
        check_vma=False,
    )
```

```python
import functools
import jax
import jax.numpy as jnp
from jax import lax
from jax.experimental import pallas as pl
from jax.experimental.pallas import tpu as pltpu
from jax.sharding import PartitionSpec as P

STEP = 0.4
BASIS = 20
QUANT = 9
ROWS = 192
LANES = 256
TRACE = 96
ELEMS = 128
SLOTS = 32
MESH = pl.DeviceIdType.MESH
F32 = jnp.float32
BF16 = jnp.bfloat16


def nn(a, b):
    return lax.dot_general(a, b, (((1,), (0,)), ((), ())), preferred_element_type=F32)


def nt(a, b):
    return lax.dot_general(a, b, (((1,), (1,)), ((), ())), preferred_element_type=F32)


def split(x):
    hi = x.astype(BF16)
    return hi, (x - hi.astype(F32)).astype(BF16)


def wide(x):
    return jnp.concatenate(split(x), axis=1)


def tall(x):
    return jnp.concatenate(split(x), axis=0)


def onehot(mask):
    return jnp.where(mask, 1.0, 0.0).astype(BF16)


def iota(shape, dim):
    return lax.broadcasted_iota(jnp.int32, shape, dim)


def triple(x):
    hi, lo = split(x)
    return jnp.concatenate([hi, lo, hi], axis=1)


def stack(pairs):
    his = [hi for hi, _ in pairs]
    return jnp.concatenate(his + his + [lo for _, lo in pairs], axis=0)


def spread(x, places):
    hi, lo = split(x)
    return nn(hi, places) + nn(lo, places)


def triple_product(x, y):
    x_hi, x_lo = split(x)
    y_hi, y_lo = split(y)
    return nn(x_hi, y_hi) + (nn(x_hi, y_lo) + nn(x_lo, y_hi))


def kron(held, left, right):
    wide_part = pl.ds(0, left.shape[1])
    for q in range(QUANT):
        held[pl.ds(BASIS * q, BASIS), wide_part] = left * right[q : q + 1]
    held[pl.ds(BASIS * QUANT, ROWS - BASIS * QUANT), wide_part] = jnp.zeros(
        (ROWS - BASIS * QUANT, left.shape[1]), F32
    )
    return held[:, wide_part]


def by_basis(index):
    return (index * 205) >> 12


def by_face_basis(index):
    return (index * 205) >> 11


def kernel(
    x_any, geo_any, clu_any, nb_any, ori_any, snd_any, st_any, sv_any, jac_any, fm_any, fp_any,
    lif_any, res_any, om_any, out_ref,
    x_in, geo_in, clu_in, nb_in, ori_in, snd_in, st_in, sv_in, jac_in, fm_in, fp_in, lif_in,
    res_in, om_in,
    x_ref, time_held, vol_held, own_held, far_held, trace_held, time_mat, vol_mat, own_mat, far_mat,
    trace_mat, near_hot, ghost_hot, outgoing, ghosts,
    in_sem, send_sem, recv_sem,
):
    pairs = [
        (x_any, x_in), (st_any, st_in), (jac_any, jac_in), (geo_any, geo_in), (snd_any, snd_in),
        (res_any, res_in), (nb_any, nb_in), (ori_any, ori_in), (sv_any, sv_in), (fm_any, fm_in),
        (lif_any, lif_in), (om_any, om_in), (fp_any, fp_in), (clu_any, clu_in),
    ]
    loads = []
    for place, (source, target) in enumerate(pairs):
        load = pltpu.make_async_copy(source, target, in_sem.at[place])
        load.start()
        loads.append(load)

    dom, sub = lax.axis_index("dom"), lax.axis_index("sub")
    doms, subs = lax.axis_size("dom"), lax.axis_size("sub")
    dom_up, dom_down = lax.rem(dom + 1, doms), lax.rem(dom + doms - 1, doms)
    sub_up, sub_down = lax.rem(sub + 1, subs), lax.rem(sub + subs - 1, subs)
    targets = [(dom_up, sub), (dom_down, sub), (dom, sub_up), (dom, sub_down)]
    below, above, left, right = dom > 0, dom < doms - 1, sub > 0, sub < subs - 1
    sends, arrives = [above, below, right, left], [below, above, left, right]
    partners = sum(exists.astype(jnp.int32) for exists in sends)
    ghosts[...] = jnp.zeros((2, ELEMS, LANES), F32)

    barrier = pltpu.get_barrier_semaphore()
    for d in range(4):
        pl.when(sends[d])(
            functools.partial(
                pl.semaphore_signal, barrier, inc=1, device_id=targets[d], device_id_type=MESH
            )
        )

    col = iota((BASIS, ROWS), 1)
    in_cols = col < BASIS * QUANT
    col_q = by_basis(col)
    col_b = col - BASIS * col_q
    basis_cols = onehot((col_b == iota((BASIS, ROWS), 0)) & in_cols)
    quant_cols = onehot((col_q == iota((BASIS, ROWS), 0)) & in_cols)[:QUANT]

    loads[1].wait()
    loads[2].wait()
    factors = jnp.concatenate([spread(jac_in[:, d, :].T, quant_cols) for d in range(3)], axis=1)
    stiff = jnp.concatenate([spread(st_in[d], basis_cols) for d in range(3)], axis=1)
    time_mat[...] = triple(kron(time_held, stiff, factors))

    loads[0].wait()
    for q in range(QUANT):
        x_ref[pl.ds(BASIS * q, BASIS), :] = x_in[q]
    x_ref[pl.ds(BASIS * QUANT, ROWS - BASIS * QUANT), :] = jnp.zeros(
        (ROWS - BASIS * QUANT, ELEMS), F32
    )
    loads[3].wait()

    def scaled_three(values):
        return stack([split(geo_in[pl.ds(g, 1), :] * values) for g in range(3)])

    def predict(values, spans):
        current = values
        sums = [(b - a) * values for a, b in spans]
        factorial = 1.0
        for degree in range(1, 4):
            current = nn(time_mat[...], scaled_three(current))
            factorial = factorial * (degree + 1)
            sign = -1.0 if degree % 2 else 1.0
            sums = [
                s + (sign * (b ** (degree + 1) - a ** (degree + 1)) / factorial) * current
                for s, (a, b) in zip(sums, spans)
            ]
        return sums

    for place in range(4, 9):
        loads[place].wait()

    trace_col = iota((10, LANES), 1)
    trace_q = by_basis(trace_col)
    for j in range(4):
        places = onehot(
            (iota((BASIS, LANES), 1) - BASIS * by_basis(iota((BASIS, LANES), 1)))
            == iota((BASIS, LANES), 0)
        )
        block = spread(res_in[:, j, :], places)
        for q in range(QUANT):
            trace_held[pl.ds(TRACE * j + 10 * q, 10), :] = jnp.where(trace_q == q, block, 0.0)
        trace_held[pl.ds(TRACE * j + 90, TRACE - 90), :] = jnp.zeros((TRACE - 90, LANES), F32)
    trace_mat[...] = triple(trace_held[...])

    facing = (ori_in[...] * 11) >> 5
    turning = ori_in[...] - 3 * facing
    behind = nb_in[...]
    near_key = jnp.where(behind < ELEMS, behind + ELEMS * facing, -1)
    key_row = iota((4 * ELEMS, ELEMS), 0)
    slot_row = iota((ELEMS, ELEMS), 0) + ELEMS
    slot_face = jnp.zeros((16, ELEMS), F32)
    for f in range(4):
        part = pl.ds(ELEMS * f, ELEMS)
        near_hot[:, part] = onehot(key_row == near_key[f : f + 1])
        hot = onehot(slot_row == behind[f : f + 1])
        ghost_hot[:, part] = hot
        face = jnp.broadcast_to(facing[f : f + 1].astype(F32), (16, ELEMS)).astype(BF16)
        slot_face = slot_face + nt(face, hot)
    slot_face = slot_face[0:1]

    stiff = jnp.concatenate([spread(sv_in[d], basis_cols) for d in range(3)], axis=1)
    vol_mat[...] = triple(kron(vol_held, stiff, factors))

    first_part, late_part = predict(x_ref[...], [(0.0, STEP), (STEP, 2.0 * STEP)])

    eye = onehot(iota((SLOTS, SLOTS), 0) == iota((SLOTS, SLOTS), 1))
    named = nt(eye, snd_in[...].astype(F32).astype(BF16))
    elem = iota((SLOTS, ELEMS), 1)
    picks = jnp.concatenate(
        [onehot(named[:, d : d + 1].astype(jnp.int32) == elem) for d in range(4)], axis=0
    )
    pick_both = jnp.concatenate([picks, picks], axis=1)

    outgoing[:, :, pl.ds(ROWS, LANES - ROWS)] = jnp.zeros((2, ELEMS, LANES - ROWS), F32)

    def send(turn, values):
        outgoing[turn, :, pl.ds(0, ROWS)] = nt(pick_both, wide(values))
        if turn == 0:
            pl.semaphore_wait(barrier, partners)
        copies = []
        for d in range(4):
            part = pl.ds(SLOTS * d, SLOTS)
            copy = pltpu.make_async_remote_copy(
                src_ref=outgoing.at[turn, part],
                dst_ref=ghosts.at[turn, part],
                send_sem=send_sem.at[turn, d],
                recv_sem=recv_sem.at[turn, d],
                device_id=targets[d],
                device_id_type=MESH,
            )
            pl.when(sends[d])(copy.start)
            copies.append(copy)
        return copies

    copies_one = send(0, first_part)

    loads[9].wait()
    loads[10].wait()
    loads[11].wait()
    loads[12].wait()
    far_col = iota((16, TRACE), 1)
    far_q = by_face_basis(far_col)
    far_row = iota((16, TRACE), 0)
    far_in = far_col < 90
    far_basis = onehot((far_col - 10 * far_q == far_row) & far_in)[:10]
    far_quant = onehot((far_q == far_row) & far_in)[:QUANT]
    turned = jnp.concatenate([spread(om_in[:, h, :], far_basis) for h in range(3)], axis=1)
    own_left, own_right, far_left, far_right = [], [], [], []
    for f in range(4):
        lifting = lif_in[:, f, :].T
        own_left.append(spread(lifting, far_basis))
        own_right.append(spread(-fm_in[:, f, :].T, far_quant))
        far_left.append(triple_product(lifting, turned))
        far_right += [spread(-fp_in[:, f, :].T, far_quant)] * 3
    own_left, own_right = jnp.concatenate(own_left, axis=1), jnp.concatenate(own_right, axis=1)
    far_left, far_right = jnp.concatenate(far_left, axis=1), jnp.concatenate(far_right, axis=1)
    own_mat[...] = triple(kron(own_held, own_left, own_right))
    far_mat[...] = triple(kron(far_held, far_left, far_right))

    def mask_of(lanes):
        piece = jnp.broadcast_to(jnp.where(lanes, 1.0, 0.0), (16, ELEMS)).astype(BF16)
        return jnp.concatenate([piece] * (TRACE // 16), axis=0)

    masks = [[mask_of(turning[f : f + 1] == h) for h in range(3)] for f in range(4)]
    scales = [geo_in[pl.ds(3 + f, 1), :] for f in range(4)]
    blank = jnp.zeros((LANES - ROWS, ELEMS), BF16)

    def correct_near(values):
        hi, lo = split(values)
        traces = nn(
            trace_mat[...], jnp.concatenate([hi, blank, hi, blank, lo, blank], axis=0)
        )
        traces = [traces[TRACE * j : TRACE * (j + 1)] for j in range(4)]
        change = nn(vol_mat[...], scaled_three(values))
        change = change + nn(own_mat[...], stack([split(scales[f] * traces[f]) for f in range(4)]))
        picked = nn(tall(jnp.concatenate(traces, axis=1)), near_hot[...])
        return change, picked[:TRACE] + picked[TRACE:]

    def correct_far(turn, picked):
        hi, lo = split(ghosts[turn])
        traces = nt(trace_mat[...], jnp.concatenate([hi, hi, lo], axis=1))
        chosen = traces[:TRACE]
        for j in range(1, 4):
            chosen = jnp.where(slot_face == j, traces[TRACE * j : TRACE * (j + 1)], chosen)
        received = nn(tall(chosen), ghost_hot[...])
        picked = picked + (received[:TRACE] + received[TRACE:])
        pairs = []
        for f in range(4):
            hi, lo = split(scales[f] * picked[:, ELEMS * f : ELEMS * (f + 1)])
            pairs += [(hi * masks[f][h], lo * masks[f][h]) for h in range(3)]
        return nn(far_mat[...], stack(pairs))

    def finish(copies):
        for d in range(4):
            pl.when(arrives[d])(copies[d].wait_recv)

    change, picked = correct_near(first_part)
    near_one = x_ref[...] + change
    finish(copies_one)
    halfway = near_one + correct_far(0, picked)
    fine_part = predict(halfway, [(0.0, STEP)])[0]
    loads[13].wait()
    second_part = jnp.where(clu_in[...] == 0, fine_part, late_part)
    copies_two = send(1, second_part)
    change, picked = correct_near(second_part)
    near_two = halfway + change
    finish(copies_two)
    x_ref[...] = near_two + correct_far(1, picked)
    for q in range(QUANT):
        out_ref[q] = x_ref[pl.ds(BASIS * q, BASIS), :]
    for copies in (copies_one, copies_two):
        for d in range(4):
            pl.when(sends[d])(copies[d].wait_send)


def local(
    solution, geometry, cluster, neighbour, orient, send_elem, stiff_time, stiff_vol, jacobians,
    flux_minus, flux_plus, lifting, restrict, orient_mat,
):
    inner = (1, 0, 2)
    args = (
        solution.transpose(inner), geometry, cluster.reshape(1, ELEMS), neighbour, orient,
        send_elem, stiff_time, stiff_vol, jacobians.transpose(inner),
        flux_minus.transpose(inner), flux_plus.transpose(inner), lifting.transpose(2, 0, 1),
        restrict.transpose(inner), orient_mat.transpose(inner),
    )
    held = [pltpu.VMEM(a.shape, a.dtype) for a in args]
    result = pl.pallas_call(
        kernel,
        out_shape=pltpu.VMEM((QUANT, BASIS, ELEMS), F32),
        in_specs=[pl.BlockSpec(memory_space=pl.ANY)] * len(args),
        out_specs=pl.BlockSpec(memory_space=pltpu.VMEM),
        scratch_shapes=held
        + [
            pltpu.VMEM((ROWS, ELEMS), F32),
            pltpu.VMEM((ROWS, 3 * ROWS), F32),
            pltpu.VMEM((ROWS, 3 * ROWS), F32),
            pltpu.VMEM((ROWS, 4 * TRACE), F32),
            pltpu.VMEM((ROWS, 12 * TRACE), F32),
            pltpu.VMEM((4 * TRACE, LANES), F32),
            pltpu.VMEM((ROWS, 9 * ROWS), BF16),
            pltpu.VMEM((ROWS, 9 * ROWS), BF16),
            pltpu.VMEM((ROWS, 12 * TRACE), BF16),
            pltpu.VMEM((ROWS, 36 * TRACE), BF16),
            pltpu.VMEM((4 * TRACE, 3 * LANES), BF16),
            pltpu.VMEM((4 * ELEMS, 4 * ELEMS), BF16),
            pltpu.VMEM((ELEMS, 4 * ELEMS), BF16),
            pltpu.VMEM((2, ELEMS, LANES), F32),
            pltpu.VMEM((2, ELEMS, LANES), F32),
            pltpu.SemaphoreType.DMA((len(args),)),
            pltpu.SemaphoreType.DMA((2, 4)),
            pltpu.SemaphoreType.DMA((2, 4)),
        ],
        compiler_params=pltpu.CompilerParams(
            collective_id=0, has_side_effects=True, vmem_limit_bytes=55 * 1024 * 1024
        ),
    )(*args)
    return result.transpose(inner)


def solution(mesh):
    split_last = P(None, ("dom", "sub"))
    return jax.shard_map(
        local,
        mesh=mesh,
        in_specs=(P(None, None, ("dom", "sub")), split_last, P(("dom", "sub")))
        + (split_last,) * 3
        + (P(),) * 8,
        out_specs=P(None, None, ("dom", "sub")),
        check_vma=False,
    )
```

```python
import functools
import jax
import jax.numpy as jnp
from jax import lax
from jax.experimental import pallas as pl
from jax.experimental.pallas import tpu as pltpu
from jax.sharding import PartitionSpec as P

STEP = 0.4
BASIS = 20
QUANT = 9
ROWS = 192
LANES = 256
TRACE = 96
ELEMS = 128
SLOTS = 32
MESH = pl.DeviceIdType.MESH
F32 = jnp.float32
BF16 = jnp.bfloat16


def nn(a, b):
    return lax.dot_general(a, b, (((1,), (0,)), ((), ())), preferred_element_type=F32)


def nt(a, b):
    return lax.dot_general(a, b, (((1,), (1,)), ((), ())), preferred_element_type=F32)


def split(x):
    hi = x.astype(BF16)
    return hi, (x - hi.astype(F32)).astype(BF16)


def wide(x):
    return jnp.concatenate(split(x), axis=1)


def tall(x):
    return jnp.concatenate(split(x), axis=0)


def onehot(mask):
    return jnp.where(mask, 1.0, 0.0).astype(BF16)


def iota(shape, dim):
    return lax.broadcasted_iota(jnp.int32, shape, dim)


def triple(x):
    hi, lo = split(x)
    return jnp.concatenate([hi, lo, hi], axis=1)


def stack(pairs):
    his = [hi for hi, _ in pairs]
    return jnp.concatenate(his + his + [lo for _, lo in pairs], axis=0)


def spread(x, places):
    hi, lo = split(x)
    return nn(hi, places) + nn(lo, places)


def triple_product(x, y):
    x_hi, x_lo = split(x)
    y_hi, y_lo = split(y)
    return nn(x_hi, y_hi) + (nn(x_hi, y_lo) + nn(x_lo, y_hi))


def kron(held, left, right):
    wide_part = pl.ds(0, left.shape[1])
    for q in range(QUANT):
        held[pl.ds(BASIS * q, BASIS), wide_part] = left * right[q : q + 1]
    held[pl.ds(BASIS * QUANT, ROWS - BASIS * QUANT), wide_part] = jnp.zeros(
        (ROWS - BASIS * QUANT, left.shape[1]), F32
    )
    return held[:, wide_part]


def by_basis(index):
    return (index * 205) >> 12


def by_face_basis(index):
    return (index * 205) >> 11


def kernel(
    x_any, geo_any, clu_any, nb_any, ori_any, snd_any, st_any, sv_any, jac_any, fm_any, fp_any,
    lif_any, res_any, om_any, out_ref,
    x_in, geo_in, clu_in, nb_in, ori_in, snd_in, st_in, sv_in, jac_in, fm_in, fp_in, lif_in,
    res_in, om_in,
    x_ref, time_held, vol_held, own_held, far_held, trace_held, time_mat, vol_mat, own_mat, far_mat,
    trace_mat, near_hot, ghost_hot, outgoing, ghosts,
    in_sem, send_sem, recv_sem,
):
    pairs = [
        (x_any, x_in), (st_any, st_in), (jac_any, jac_in), (geo_any, geo_in), (snd_any, snd_in),
        (res_any, res_in), (nb_any, nb_in), (ori_any, ori_in), (sv_any, sv_in), (fm_any, fm_in),
        (lif_any, lif_in), (om_any, om_in), (fp_any, fp_in), (clu_any, clu_in),
    ]
    loads = []
    for place, (source, target) in enumerate(pairs):
        load = pltpu.make_async_copy(source, target, in_sem.at[place])
        load.start()
        loads.append(load)

    dom, sub = lax.axis_index("dom"), lax.axis_index("sub")
    doms, subs = lax.axis_size("dom"), lax.axis_size("sub")
    dom_up, dom_down = lax.rem(dom + 1, doms), lax.rem(dom + doms - 1, doms)
    sub_up, sub_down = lax.rem(sub + 1, subs), lax.rem(sub + subs - 1, subs)
    targets = [(dom_up, sub), (dom_down, sub), (dom, sub_up), (dom, sub_down)]
    below, above, left, right = dom > 0, dom < doms - 1, sub > 0, sub < subs - 1
    sends, arrives = [above, below, right, left], [below, above, left, right]
    partners = sum(exists.astype(jnp.int32) for exists in sends)
    ghosts[...] = jnp.zeros((2, ELEMS, LANES), F32)

    barrier = pltpu.get_barrier_semaphore()
    for d in range(4):
        pl.when(sends[d])(
            functools.partial(
                pl.semaphore_signal, barrier, inc=1, device_id=targets[d], device_id_type=MESH
            )
        )

    col = iota((BASIS, ROWS), 1)
    in_cols = col < BASIS * QUANT
    col_q = by_basis(col)
    col_b = col - BASIS * col_q
    basis_cols = onehot((col_b == iota((BASIS, ROWS), 0)) & in_cols)
    quant_cols = onehot((col_q == iota((BASIS, ROWS), 0)) & in_cols)[:QUANT]

    loads[1].wait()
    loads[2].wait()
    factors = jnp.concatenate([spread(jac_in[:, d, :].T, quant_cols) for d in range(3)], axis=1)
    stiff = jnp.concatenate([spread(st_in[d], basis_cols) for d in range(3)], axis=1)
    time_mat[...] = triple(kron(time_held, stiff, factors))

    loads[0].wait()
    for q in range(QUANT):
        x_ref[pl.ds(BASIS * q, BASIS), :] = x_in[q]
    x_ref[pl.ds(BASIS * QUANT, ROWS - BASIS * QUANT), :] = jnp.zeros(
        (ROWS - BASIS * QUANT, ELEMS), F32
    )
    loads[3].wait()

    def scaled_three(values):
        return stack([split(geo_in[pl.ds(g, 1), :] * values) for g in range(3)])

    def predict(values, spans):
        current = values
        sums = [(b - a) * values for a, b in spans]
        factorial = 1.0
        for degree in range(1, 4):
            current = nn(time_mat[...], scaled_three(current))
            factorial = factorial * (degree + 1)
            sign = -1.0 if degree % 2 else 1.0
            sums = [
                s + (sign * (b ** (degree + 1) - a ** (degree + 1)) / factorial) * current
                for s, (a, b) in zip(sums, spans)
            ]
        return sums

    for place in range(4, 9):
        loads[place].wait()

    trace_col = iota((10, LANES), 1)
    trace_q = by_basis(trace_col)
    for j in range(4):
        places = onehot(
            (iota((BASIS, LANES), 1) - BASIS * by_basis(iota((BASIS, LANES), 1)))
            == iota((BASIS, LANES), 0)
        )
        block = spread(res_in[:, j, :], places)
        for q in range(QUANT):
            trace_held[pl.ds(TRACE * j + 10 * q, 10), :] = jnp.where(trace_q == q, block, 0.0)
        trace_held[pl.ds(TRACE * j + 90, TRACE - 90), :] = jnp.zeros((TRACE - 90, LANES), F32)
    trace_mat[...] = triple(trace_held[...])

    facing = (ori_in[...] * 11) >> 5
    turning = ori_in[...] - 3 * facing
    behind = nb_in[...]
    near_key = jnp.where(behind < ELEMS, behind + ELEMS * facing, -1)
    key_row = iota((4 * ELEMS, ELEMS), 0)
    slot_row = iota((ELEMS, ELEMS), 0) + ELEMS
    info_row = iota((16, ELEMS), 0)
    slot_info = jnp.zeros((16, ELEMS), F32)
    slot_hot = jnp.zeros((ELEMS, ELEMS), F32)
    for f in range(4):
        near_hot[:, pl.ds(ELEMS * f, ELEMS)] = onehot(key_row == near_key[f : f + 1])
        hot = jnp.where(slot_row == behind[f : f + 1], 1.0, 0.0)
        slot_hot = slot_hot + hot
        ghost_hot[:, pl.ds(ELEMS * f, ELEMS)] = hot.astype(BF16)
        scale = geo_in[pl.ds(3 + f, 1), :]
        scale_hi = scale.astype(BF16).astype(F32)
        scale_mid = (scale - scale_hi).astype(BF16).astype(F32)
        info = jnp.where(info_row == 0, facing[f : f + 1].astype(F32), 0.0)
        info = jnp.where(info_row == 1, (3 * f + turning[f : f + 1]).astype(F32), info)
        info = jnp.where(info_row == 2, scale_hi, info)
        info = jnp.where(info_row == 3, scale_mid, info)
        info = jnp.where(info_row == 4, scale - scale_hi - scale_mid, info)
        slot_info = slot_info + nt(info.astype(BF16), hot.astype(BF16))
    slot_hot = slot_hot.astype(BF16)
    slot_both = jnp.concatenate([slot_hot, slot_hot], axis=0)
    slot_face, slot_kind = slot_info[0:1], slot_info[1:2]
    slot_scale = slot_info[2:3] + slot_info[3:4] + slot_info[4:5]

    stiff = jnp.concatenate([spread(sv_in[d], basis_cols) for d in range(3)], axis=1)
    vol_mat[...] = triple(kron(vol_held, stiff, factors))

    first_part, late_part = predict(x_ref[...], [(0.0, STEP), (STEP, 2.0 * STEP)])

    eye = onehot(iota((SLOTS, SLOTS), 0) == iota((SLOTS, SLOTS), 1))
    named = nt(eye, snd_in[...].astype(F32).astype(BF16))
    elem = iota((SLOTS, ELEMS), 1)
    picks = jnp.concatenate(
        [onehot(named[:, d : d + 1].astype(jnp.int32) == elem) for d in range(4)], axis=0
    )
    pick_both = jnp.concatenate([picks, picks], axis=1)

    outgoing[:, :, pl.ds(ROWS, LANES - ROWS)] = jnp.zeros((2, ELEMS, LANES - ROWS), F32)

    def send(turn, values):
        outgoing[turn, :, pl.ds(0, ROWS)] = nt(pick_both, wide(values))
        if turn == 0:
            pl.semaphore_wait(barrier, partners)
        copies = []
        for d in range(4):
            part = pl.ds(SLOTS * d, SLOTS)
            copy = pltpu.make_async_remote_copy(
                src_ref=outgoing.at[turn, part],
                dst_ref=ghosts.at[turn, part],
                send_sem=send_sem.at[turn, d],
                recv_sem=recv_sem.at[turn, d],
                device_id=targets[d],
                device_id_type=MESH,
            )
            pl.when(sends[d])(copy.start)
            copies.append(copy)
        return copies

    copies_one = send(0, first_part)

    loads[9].wait()
    loads[10].wait()
    loads[11].wait()
    loads[12].wait()
    far_col = iota((16, TRACE), 1)
    far_q = by_face_basis(far_col)
    far_row = iota((16, TRACE), 0)
    far_in = far_col < 90
    far_basis = onehot((far_col - 10 * far_q == far_row) & far_in)[:10]
    far_quant = onehot((far_q == far_row) & far_in)[:QUANT]
    turned = jnp.concatenate([spread(om_in[:, h, :], far_basis) for h in range(3)], axis=1)
    own_left, own_right, far_left, far_right = [], [], [], []
    for f in range(4):
        lifting = lif_in[:, f, :].T
        own_left.append(spread(lifting, far_basis))
        own_right.append(spread(-fm_in[:, f, :].T, far_quant))
        far_left.append(triple_product(lifting, turned))
        far_right += [spread(-fp_in[:, f, :].T, far_quant)] * 3
    own_left, own_right = jnp.concatenate(own_left, axis=1), jnp.concatenate(own_right, axis=1)
    far_left, far_right = jnp.concatenate(far_left, axis=1), jnp.concatenate(far_right, axis=1)
    own_mat[...] = triple(kron(own_held, own_left, own_right))
    far_mat[...] = triple(kron(far_held, far_left, far_right))

    def mask_of(lanes):
        piece = jnp.broadcast_to(jnp.where(lanes, 1.0, 0.0), (16, ELEMS)).astype(BF16)
        return jnp.concatenate([piece] * (TRACE // 16), axis=0)

    masks = [[mask_of(turning[f : f + 1] == h) for h in range(3)] for f in range(4)]
    slot_masks = [mask_of(slot_kind == float(kind)) for kind in range(12)]
    scales = [geo_in[pl.ds(3 + f, 1), :] for f in range(4)]
    blank = jnp.zeros((LANES - ROWS, ELEMS), BF16)

    def correct_near(values):
        hi, lo = split(values)
        traces = nn(
            trace_mat[...], jnp.concatenate([hi, blank, hi, blank, lo, blank], axis=0)
        )
        traces = [traces[TRACE * j : TRACE * (j + 1)] for j in range(4)]
        change = nn(vol_mat[...], scaled_three(values))
        change = change + nn(own_mat[...], stack([split(scales[f] * traces[f]) for f in range(4)]))
        picked = nn(tall(jnp.concatenate(traces, axis=1)), near_hot[...])
        return change, picked[:TRACE] + picked[TRACE:]

    def flux_behind(picked):
        pairs = []
        for f in range(4):
            hi, lo = split(scales[f] * picked[:, ELEMS * f : ELEMS * (f + 1)])
            pairs += [(hi * masks[f][h], lo * masks[f][h]) for h in range(3)]
        return nn(far_mat[...], stack(pairs))

    def slot_traces(turn):
        hi, lo = split(ghosts[turn])
        traces = nt(trace_mat[...], jnp.concatenate([hi, hi, lo], axis=1))
        chosen = traces[:TRACE]
        for j in range(1, 4):
            chosen = jnp.where(slot_face == j, traces[TRACE * j : TRACE * (j + 1)], chosen)
        return chosen

    def correct_joined(turn, picked):
        received = nn(tall(slot_traces(turn)), ghost_hot[...])
        return flux_behind(picked + (received[:TRACE] + received[TRACE:]))

    def correct_slots(turn):
        hi, lo = split(slot_scale * slot_traces(turn))
        lifted = nn(far_mat[...], stack([(hi * mask, lo * mask) for mask in slot_masks]))
        return nn(wide(lifted), slot_both)

    def finish(copies):
        for d in range(4):
            pl.when(arrives[d])(copies[d].wait_recv)

    change, picked = correct_near(first_part)
    near_one = x_ref[...] + change
    finish(copies_one)
    halfway = near_one + correct_joined(0, picked)
    fine_part = predict(halfway, [(0.0, STEP)])[0]
    loads[13].wait()
    second_part = jnp.where(clu_in[...] == 0, fine_part, late_part)
    copies_two = send(1, second_part)
    change, picked = correct_near(second_part)
    near_two = halfway + change + flux_behind(picked)
    finish(copies_two)
    x_ref[...] = near_two + correct_slots(1)
    for q in range(QUANT):
        out_ref[q] = x_ref[pl.ds(BASIS * q, BASIS), :]
    for copies in (copies_one, copies_two):
        for d in range(4):
            pl.when(sends[d])(copies[d].wait_send)


def local(
    solution, geometry, cluster, neighbour, orient, send_elem, stiff_time, stiff_vol, jacobians,
    flux_minus, flux_plus, lifting, restrict, orient_mat,
):
    inner = (1, 0, 2)
    args = (
        solution.transpose(inner), geometry, cluster.reshape(1, ELEMS), neighbour, orient,
        send_elem, stiff_time, stiff_vol, jacobians.transpose(inner),
        flux_minus.transpose(inner), flux_plus.transpose(inner), lifting.transpose(2, 0, 1),
        restrict.transpose(inner), orient_mat.transpose(inner),
    )
    held = [pltpu.VMEM(a.shape, a.dtype) for a in args]
    result = pl.pallas_call(
        kernel,
        out_shape=pltpu.VMEM((QUANT, BASIS, ELEMS), F32),
        in_specs=[pl.BlockSpec(memory_space=pl.ANY)] * len(args),
        out_specs=pl.BlockSpec(memory_space=pltpu.VMEM),
        scratch_shapes=held
        + [
            pltpu.VMEM((ROWS, ELEMS), F32),
            pltpu.VMEM((ROWS, 3 * ROWS), F32),
            pltpu.VMEM((ROWS, 3 * ROWS), F32),
            pltpu.VMEM((ROWS, 4 * TRACE), F32),
            pltpu.VMEM((ROWS, 12 * TRACE), F32),
            pltpu.VMEM((4 * TRACE, LANES), F32),
            pltpu.VMEM((ROWS, 9 * ROWS), BF16),
            pltpu.VMEM((ROWS, 9 * ROWS), BF16),
            pltpu.VMEM((ROWS, 12 * TRACE), BF16),
            pltpu.VMEM((ROWS, 36 * TRACE), BF16),
            pltpu.VMEM((4 * TRACE, 3 * LANES), BF16),
            pltpu.VMEM((4 * ELEMS, 4 * ELEMS), BF16),
            pltpu.VMEM((ELEMS, 4 * ELEMS), BF16),
            pltpu.VMEM((2, ELEMS, LANES), F32),
            pltpu.VMEM((2, ELEMS, LANES), F32),
            pltpu.SemaphoreType.DMA((len(args),)),
            pltpu.SemaphoreType.DMA((2, 4)),
            pltpu.SemaphoreType.DMA((2, 4)),
        ],
        compiler_params=pltpu.CompilerParams(
            collective_id=0, has_side_effects=True, vmem_limit_bytes=55 * 1024 * 1024
        ),
    )(*args)
    return result.transpose(inner)


def solution(mesh):
    split_last = P(None, ("dom", "sub"))
    return jax.shard_map(
        local,
        mesh=mesh,
        in_specs=(P(None, None, ("dom", "sub")), split_last, P(("dom", "sub")))
        + (split_last,) * 3
        + (P(),) * 8,
        out_specs=P(None, None, ("dom", "sub")),
        check_vma=False,
    )
```

```python
import functools
import jax
import jax.numpy as jnp
from jax import lax
from jax.experimental import pallas as pl
from jax.experimental.pallas import tpu as pltpu
from jax.sharding import PartitionSpec as P

STEP = 0.4
BASIS = 20
QUANT = 9
ROWS = 192
LANES = 256
TRACE = 96
ELEMS = 128
SLOTS = 32
MESH = pl.DeviceIdType.MESH
F32 = jnp.float32
BF16 = jnp.bfloat16


def nn(a, b):
    return lax.dot_general(a, b, (((1,), (0,)), ((), ())), preferred_element_type=F32)


def nt(a, b):
    return lax.dot_general(a, b, (((1,), (1,)), ((), ())), preferred_element_type=F32)


def split(x):
    hi = x.astype(BF16)
    return hi, (x - hi.astype(F32)).astype(BF16)


def wide(x):
    return jnp.concatenate(split(x), axis=1)


def tall(x):
    return jnp.concatenate(split(x), axis=0)


def onehot(mask):
    return jnp.where(mask, 1.0, 0.0).astype(BF16)


def iota(shape, dim):
    return lax.broadcasted_iota(jnp.int32, shape, dim)


def triple(x):
    hi, lo = split(x)
    return jnp.concatenate([hi, lo, hi], axis=1)


def stack(pairs):
    his = [hi for hi, _ in pairs]
    return jnp.concatenate(his + his + [lo for _, lo in pairs], axis=0)


def spread(x, places):
    hi, lo = split(x)
    return nn(hi, places) + nn(lo, places)


def triple_product(x, y):
    x_hi, x_lo = split(x)
    y_hi, y_lo = split(y)
    return nn(x_hi, y_hi) + (nn(x_hi, y_lo) + nn(x_lo, y_hi))


def kron(held, left, right):
    wide_part = pl.ds(0, left.shape[1])
    for q in range(QUANT):
        held[pl.ds(BASIS * q, BASIS), wide_part] = left * right[q : q + 1]
    held[pl.ds(BASIS * QUANT, ROWS - BASIS * QUANT), wide_part] = jnp.zeros(
        (ROWS - BASIS * QUANT, left.shape[1]), F32
    )
    return held[:, wide_part]


def by_basis(index):
    return (index * 205) >> 12


def by_face_basis(index):
    return (index * 205) >> 11


def kernel(
    x_any, geo_any, clu_any, nb_any, ori_any, snd_any, st_any, sv_any, jac_any, fm_any, fp_any,
    lif_any, res_any, om_any, out_ref,
    x_in, geo_in, clu_in, nb_in, ori_in, snd_in, st_in, sv_in, jac_in, fm_in, fp_in, lif_in,
    res_in, om_in,
    x_ref, time_held, vol_held, own_held, far_held, trace_held, time_mat, vol_mat, own_mat, far_mat,
    trace_mat, near_hot, ghost_hot, outgoing, ghosts,
    in_sem, send_sem, recv_sem,
):
    pairs = [
        (x_any, x_in), (st_any, st_in), (jac_any, jac_in), (geo_any, geo_in), (snd_any, snd_in),
        (res_any, res_in), (nb_any, nb_in), (ori_any, ori_in), (sv_any, sv_in), (fm_any, fm_in),
        (lif_any, lif_in), (om_any, om_in), (fp_any, fp_in), (clu_any, clu_in),
    ]
    loads = []
    for place, (source, target) in enumerate(pairs):
        load = pltpu.make_async_copy(source, target, in_sem.at[place])
        load.start()
        loads.append(load)

    dom, sub = lax.axis_index("dom"), lax.axis_index("sub")
    doms, subs = lax.axis_size("dom"), lax.axis_size("sub")
    dom_up, dom_down = lax.rem(dom + 1, doms), lax.rem(dom + doms - 1, doms)
    sub_up, sub_down = lax.rem(sub + 1, subs), lax.rem(sub + subs - 1, subs)
    targets = [(dom_up, sub), (dom_down, sub), (dom, sub_up), (dom, sub_down)]
    below, above, left, right = dom > 0, dom < doms - 1, sub > 0, sub < subs - 1
    sends, arrives = [above, below, right, left], [below, above, left, right]
    partners = sum(exists.astype(jnp.int32) for exists in sends)
    ghosts[...] = jnp.zeros((2, ELEMS, LANES), F32)

    barrier = pltpu.get_barrier_semaphore()
    for d in range(4):
        pl.when(sends[d])(
            functools.partial(
                pl.semaphore_signal, barrier, inc=1, device_id=targets[d], device_id_type=MESH
            )
        )

    col = iota((BASIS, ROWS), 1)
    in_cols = col < BASIS * QUANT
    col_q = by_basis(col)
    col_b = col - BASIS * col_q
    basis_cols = onehot((col_b == iota((BASIS, ROWS), 0)) & in_cols)
    quant_cols = onehot((col_q == iota((BASIS, ROWS), 0)) & in_cols)[:QUANT]

    loads[1].wait()
    loads[2].wait()
    factors = jnp.concatenate([spread(jac_in[:, d, :].T, quant_cols) for d in range(3)], axis=1)
    stiff = jnp.concatenate([spread(st_in[d], basis_cols) for d in range(3)], axis=1)
    time_mat[...] = triple(kron(time_held, stiff, factors))

    loads[0].wait()
    for q in range(QUANT):
        x_ref[pl.ds(BASIS * q, BASIS), :] = x_in[q]
    x_ref[pl.ds(BASIS * QUANT, ROWS - BASIS * QUANT), :] = jnp.zeros(
        (ROWS - BASIS * QUANT, ELEMS), F32
    )
    loads[3].wait()

    def scaled_three(values):
        return stack([split(geo_in[pl.ds(g, 1), :] * values) for g in range(3)])

    def predict(values, spans):
        current = values
        sums = [(b - a) * values for a, b in spans]
        factorial = 1.0
        for degree in range(1, 4):
            current = nn(time_mat[...], scaled_three(current))
            factorial = factorial * (degree + 1)
            sign = -1.0 if degree % 2 else 1.0
            sums = [
                s + (sign * (b ** (degree + 1) - a ** (degree + 1)) / factorial) * current
                for s, (a, b) in zip(sums, spans)
            ]
        return sums

    first_part, late_part = predict(x_ref[...], [(0.0, STEP), (STEP, 2.0 * STEP)])

    loads[4].wait()
    eye = onehot(iota((SLOTS, SLOTS), 0) == iota((SLOTS, SLOTS), 1))
    named = nt(eye, snd_in[...].astype(F32).astype(BF16))
    elem = iota((SLOTS, ELEMS), 1)
    picks = jnp.concatenate(
        [onehot(named[:, d : d + 1].astype(jnp.int32) == elem) for d in range(4)], axis=0
    )
    pick_both = jnp.concatenate([picks, picks], axis=1)

    outgoing[:, :, pl.ds(ROWS, LANES - ROWS)] = jnp.zeros((2, ELEMS, LANES - ROWS), F32)

    def send(turn, values):
        outgoing[turn, :, pl.ds(0, ROWS)] = nt(pick_both, wide(values))
        if turn == 0:
            pl.semaphore_wait(barrier, partners)
        copies = []
        for d in range(4):
            part = pl.ds(SLOTS * d, SLOTS)
            copy = pltpu.make_async_remote_copy(
                src_ref=outgoing.at[turn, part],
                dst_ref=ghosts.at[turn, part],
                send_sem=send_sem.at[turn, d],
                recv_sem=recv_sem.at[turn, d],
                device_id=targets[d],
                device_id_type=MESH,
            )
            pl.when(sends[d])(copy.start)
            copies.append(copy)
        return copies

    copies_one = send(0, first_part)

    for place in range(5, 9):
        loads[place].wait()

    trace_col = iota((10, LANES), 1)
    trace_q = by_basis(trace_col)
    for j in range(4):
        places = onehot(
            (iota((BASIS, LANES), 1) - BASIS * by_basis(iota((BASIS, LANES), 1)))
            == iota((BASIS, LANES), 0)
        )
        block = spread(res_in[:, j, :], places)
        for q in range(QUANT):
            trace_held[pl.ds(TRACE * j + 10 * q, 10), :] = jnp.where(trace_q == q, block, 0.0)
        trace_held[pl.ds(TRACE * j + 90, TRACE - 90), :] = jnp.zeros((TRACE - 90, LANES), F32)
    trace_mat[...] = triple(trace_held[...])

    facing = (ori_in[...] * 11) >> 5
    turning = ori_in[...] - 3 * facing
    behind = nb_in[...]
    near_key = jnp.where(behind < ELEMS, behind + ELEMS * facing, -1)
    key_row = iota((4 * ELEMS, ELEMS), 0)
    slot_row = iota((ELEMS, ELEMS), 0) + ELEMS
    info_row = iota((16, ELEMS), 0)
    slot_info = jnp.zeros((16, ELEMS), F32)
    slot_hot = jnp.zeros((ELEMS, ELEMS), F32)
    for f in range(4):
        near_hot[:, pl.ds(ELEMS * f, ELEMS)] = onehot(key_row == near_key[f : f + 1])
        hot = jnp.where(slot_row == behind[f : f + 1], 1.0, 0.0)
        slot_hot = slot_hot + hot
        ghost_hot[:, pl.ds(ELEMS * f, ELEMS)] = hot.astype(BF16)
        scale = geo_in[pl.ds(3 + f, 1), :]
        scale_hi = scale.astype(BF16).astype(F32)
        scale_mid = (scale - scale_hi).astype(BF16).astype(F32)
        info = jnp.where(info_row == 0, facing[f : f + 1].astype(F32), 0.0)
        info = jnp.where(info_row == 1, (3 * f + turning[f : f + 1]).astype(F32), info)
        info = jnp.where(info_row == 2, scale_hi, info)
        info = jnp.where(info_row == 3, scale_mid, info)
        info = jnp.where(info_row == 4, scale - scale_hi - scale_mid, info)
        slot_info = slot_info + nt(info.astype(BF16), hot.astype(BF16))
    slot_hot = slot_hot.astype(BF16)
    slot_both = jnp.concatenate([slot_hot, slot_hot], axis=0)
    slot_face, slot_kind = slot_info[0:1], slot_info[1:2]
    slot_scale = slot_info[2:3] + slot_info[3:4] + slot_info[4:5]

    stiff = jnp.concatenate([spread(sv_in[d], basis_cols) for d in range(3)], axis=1)
    vol_mat[...] = triple(kron(vol_held, stiff, factors))

    loads[9].wait()
    loads[10].wait()
    loads[11].wait()
    loads[12].wait()
    far_col = iota((16, TRACE), 1)
    far_q = by_face_basis(far_col)
    far_row = iota((16, TRACE), 0)
    far_in = far_col < 90
    far_basis = onehot((far_col - 10 * far_q == far_row) & far_in)[:10]
    far_quant = onehot((far_q == far_row) & far_in)[:QUANT]
    turned = jnp.concatenate([spread(om_in[:, h, :], far_basis) for h in range(3)], axis=1)
    own_left, own_right, far_left, far_right = [], [], [], []
    for f in range(4):
        lifting = lif_in[:, f, :].T
        own_left.append(spread(lifting, far_basis))
        own_right.append(spread(-fm_in[:, f, :].T, far_quant))
        far_left.append(triple_product(lifting, turned))
        far_right += [spread(-fp_in[:, f, :].T, far_quant)] * 3
    own_left, own_right = jnp.concatenate(own_left, axis=1), jnp.concatenate(own_right, axis=1)
    far_left, far_right = jnp.concatenate(far_left, axis=1), jnp.concatenate(far_right, axis=1)
    own_mat[...] = triple(kron(own_held, own_left, own_right))
    far_mat[...] = triple(kron(far_held, far_left, far_right))

    def mask_of(lanes):
        piece = jnp.broadcast_to(jnp.where(lanes, 1.0, 0.0), (16, ELEMS)).astype(BF16)
        return jnp.concatenate([piece] * (TRACE // 16), axis=0)

    masks = [[mask_of(turning[f : f + 1] == h) for h in range(3)] for f in range(4)]
    slot_masks = [mask_of(slot_kind == float(kind)) for kind in range(12)]
    scales = [geo_in[pl.ds(3 + f, 1), :] for f in range(4)]
    blank = jnp.zeros((LANES - ROWS, ELEMS), BF16)

    def correct_near(values):
        hi, lo = split(values)
        traces = nn(
            trace_mat[...], jnp.concatenate([hi, blank, hi, blank, lo, blank], axis=0)
        )
        traces = [traces[TRACE * j : TRACE * (j + 1)] for j in range(4)]
        change = nn(vol_mat[...], scaled_three(values))
        change = change + nn(own_mat[...], stack([split(scales[f] * traces[f]) for f in range(4)]))
        picked = nn(tall(jnp.concatenate(traces, axis=1)), near_hot[...])
        return change, picked[:TRACE] + picked[TRACE:]

    def flux_behind(picked):
        pairs = []
        for f in range(4):
            hi, lo = split(scales[f] * picked[:, ELEMS * f : ELEMS * (f + 1)])
            pairs += [(hi * masks[f][h], lo * masks[f][h]) for h in range(3)]
        return nn(far_mat[...], stack(pairs))

    def slot_traces(turn):
        hi, lo = split(ghosts[turn])
        traces = nt(trace_mat[...], jnp.concatenate([hi, hi, lo], axis=1))
        chosen = traces[:TRACE]
        for j in range(1, 4):
            chosen = jnp.where(slot_face == j, traces[TRACE * j : TRACE * (j + 1)], chosen)
        return chosen

    def correct_joined(turn, picked):
        received = nn(tall(slot_traces(turn)), ghost_hot[...])
        return flux_behind(picked + (received[:TRACE] + received[TRACE:]))

    def correct_slots(turn):
        hi, lo = split(slot_scale * slot_traces(turn))
        lifted = nn(far_mat[...], stack([(hi * mask, lo * mask) for mask in slot_masks]))
        return nn(wide(lifted), slot_both)

    def finish(copies):
        for d in range(4):
            pl.when(arrives[d])(copies[d].wait_recv)

    change, picked = correct_near(first_part)
    near_one = x_ref[...] + change
    finish(copies_one)
    halfway = near_one + correct_joined(0, picked)
    fine_part = predict(halfway, [(0.0, STEP)])[0]
    loads[13].wait()
    second_part = jnp.where(clu_in[...] == 0, fine_part, late_part)
    copies_two = send(1, second_part)
    change, picked = correct_near(second_part)
    near_two = halfway + change + flux_behind(picked)
    finish(copies_two)
    x_ref[...] = near_two + correct_slots(1)
    for q in range(QUANT):
        out_ref[q] = x_ref[pl.ds(BASIS * q, BASIS), :]
    for copies in (copies_one, copies_two):
        for d in range(4):
            pl.when(sends[d])(copies[d].wait_send)


def local(
    solution, geometry, cluster, neighbour, orient, send_elem, stiff_time, stiff_vol, jacobians,
    flux_minus, flux_plus, lifting, restrict, orient_mat,
):
    inner = (1, 0, 2)
    args = (
        solution.transpose(inner), geometry, cluster.reshape(1, ELEMS), neighbour, orient,
        send_elem, stiff_time, stiff_vol, jacobians.transpose(inner),
        flux_minus.transpose(inner), flux_plus.transpose(inner), lifting.transpose(2, 0, 1),
        restrict.transpose(inner), orient_mat.transpose(inner),
    )
    held = [pltpu.VMEM(a.shape, a.dtype) for a in args]
    result = pl.pallas_call(
        kernel,
        out_shape=pltpu.VMEM((QUANT, BASIS, ELEMS), F32),
        in_specs=[pl.BlockSpec(memory_space=pl.ANY)] * len(args),
        out_specs=pl.BlockSpec(memory_space=pltpu.VMEM),
        scratch_shapes=held
        + [
            pltpu.VMEM((ROWS, ELEMS), F32),
            pltpu.VMEM((ROWS, 3 * ROWS), F32),
            pltpu.VMEM((ROWS, 3 * ROWS), F32),
            pltpu.VMEM((ROWS, 4 * TRACE), F32),
            pltpu.VMEM((ROWS, 12 * TRACE), F32),
            pltpu.VMEM((4 * TRACE, LANES), F32),
            pltpu.VMEM((ROWS, 9 * ROWS), BF16),
            pltpu.VMEM((ROWS, 9 * ROWS), BF16),
            pltpu.VMEM((ROWS, 12 * TRACE), BF16),
            pltpu.VMEM((ROWS, 36 * TRACE), BF16),
            pltpu.VMEM((4 * TRACE, 3 * LANES), BF16),
            pltpu.VMEM((4 * ELEMS, 4 * ELEMS), BF16),
            pltpu.VMEM((ELEMS, 4 * ELEMS), BF16),
            pltpu.VMEM((2, ELEMS, LANES), F32),
            pltpu.VMEM((2, ELEMS, LANES), F32),
            pltpu.SemaphoreType.DMA((len(args),)),
            pltpu.SemaphoreType.DMA((2, 4)),
            pltpu.SemaphoreType.DMA((2, 4)),
        ],
        compiler_params=pltpu.CompilerParams(
            collective_id=0, has_side_effects=True, vmem_limit_bytes=55 * 1024 * 1024
        ),
    )(*args)
    return result.transpose(inner)


def solution(mesh):
    split_last = P(None, ("dom", "sub"))
    return jax.shard_map(
        local,
        mesh=mesh,
        in_specs=(P(None, None, ("dom", "sub")), split_last, P(("dom", "sub")))
        + (split_last,) * 3
        + (P(),) * 8,
        out_specs=P(None, None, ("dom", "sub")),
        check_vma=False,
    )
```
